32 devices in a mesh: dp: 2 (over x), expert: 4 (over z), hidden: 4 (over y, core).
Axes of the slice: x: 2, y: 2, z: 4, core: 2. Of those that a mesh axis runs over, the one named last changes fastest.
Arguments:
- tokens: bfloat16 [16384, 1152], P(('dp', 'expert', 'hidden')), may hold values from -6 to 6
- route: int32 [16384, 1], P(('dp', 'expert', 'hidden')), may hold values from 0 to 3; in each aligned block of 512 rows (0 to 511, 512 to 1023, ...) at most 256 rows name the same one
- norm_gain: bfloat16 [1152], replicated, may hold values from 0.5 to 1.5
- router_weight: bfloat16 [1152, 4], replicated, may hold values from -0.119628906 to 0.119628906
- w_in: bfloat16 [4, 1152, 3072], P('expert', None, 'hidden'), may hold values from -0.1875 to 0.1875
- w_out: bfloat16 [4, 3072, 1152], P('expert', 'hidden'), may hold values from -0.8984375 to 0.8984375
- cotangent: bfloat16 [16384, 1152], P(('dp', 'expert', 'hidden')), may hold values from -6 to 6
Outputs:
- activations: bfloat16 [16384, 1152], P(('dp', 'expert', 'hidden'))
- input_grad: float32 [16384, 1152], P(('dp', 'expert', 'hidden'))
- gain_grad: float32 [1152], replicated
- router_grad: float32 [1152, 4], replicated
- w_in_grad: float32 [4, 1152, 3072], P('expert', None, 'hidden')
- w_out_grad: float32 [4, 3072, 1152], P('expert', 'hidden')
The draws below stay inside these ranges and needn't reach their ends.
Inputs may be any that keep to these rules, and one draw needn't show every extreme that they name: `route`: in the rows of one device (aligned blocks of 512 rows) no expert is named more than 256 times, a bound that some block reaches; every expert is named somewhere.
All inputs are finite; a program needn't handle non-finite values.
Results may differ from the reference program's by a relative error of at most 0.0068.
Values may be sent and summed in bfloat16 or wider, within the bound.
A program may use at most 192 MiB of HBM per device.

```python
import math
import jax
import jax.numpy as jnp
import numpy as np
from jax import lax

D = 1152
FF = 3072
TOK_DEV = 512
EXPERTS = 4
TOKENS = 16384
CAP = 256


def levels(rng, extent, shards, least, top_value):
    level = 1.0
    for position, blocks in shards:
        draws = jax.random.uniform(jax.random.fold_in(jax.random.fold_in(rng, 6), position), (blocks,), jnp.float32, least / len(shards), top_value / len(shards))
        level = level * jnp.repeat(jnp.exp(draws), extent[position] // blocks).reshape((-1,) + (1,) * (len(extent) - 1 - position))
    return level


def routed_block(key, own, number, rows, amount, top, reach, slope):
    order = jax.random.permutation(key, amount)
    heavy_load, ordinary = portions_of(amount, rows * top, reach, slope, True), portions_of(amount, rows * top, reach, slope, False)
    places = jnp.arange(amount)

    def named(tallies, turn):
        used = int((tallies > 0).sum())
        fixed = max(1, used // 4)
        moved = fixed + (places - fixed + turn * (used - fixed)) % max(1, amount - fixed)
        return jnp.zeros((amount,), jnp.int32).at[order[jnp.where(places < fixed, places, moved)]].set(jnp.asarray(tallies, jnp.int32))

    tallies = jnp.where(number % 4 == 0, named(heavy_load, number // 4), named(ordinary, number - number // 4 - 1))
    mixed = jax.random.permutation(jax.random.fold_in(own, 3), amount)
    source_of, taker = mixed[0:amount // 2 * 2:2], mixed[1:amount // 2 * 2:2]
    slack = jnp.minimum(tallies[source_of] - 1, reach - tallies[taker]) // 2
    slack = jnp.where((source_of == order[0]) | (taker == order[0]) | (tallies[taker] == 0), 0, jnp.maximum(slack, 0))
    moved = jax.random.randint(jax.random.fold_in(own, 4), (amount // 2,), 0, 1 << 20) % (slack + 1)
    tallies = tallies.at[source_of].add(-moved).at[taker].add(moved)
    items = jnp.searchsorted(jnp.cumsum(tallies), jnp.arange(rows * top), side="right").astype(jnp.int32)
    table = items.reshape(top, rows).T
    table = table[jax.random.permutation(jax.random.fold_in(own, 1), rows)]
    turn = jax.random.randint(jax.random.fold_in(own, 2), (rows, 1), 0, top)
    return jnp.take_along_axis(table, (jnp.arange(top)[None, :] + turn) % top, axis=1)


def portions_of(number_of, total, most, lean, full):
    portions = [(1 << 20) // math.isqrt(rank ** lean) + 1 for rank in range(1, number_of + 1)]
    largest = most if full else min(most, max(-(-total // number_of), total * portions[0] // sum(portions)))
    least = 1 if total - largest >= number_of - 1 else 0
    holding, rest = [largest] + [least] * (number_of - 1), total - largest - least * (number_of - 1)
    while rest > 0:
        movable = [i for i in range(1, number_of) if holding[i] < largest] or [i for i in range(1, number_of) if holding[i] < most]
        whole, remaining = sum([portions[i] for i in movable]), rest
        for i in movable:
            extra = min(most - holding[i], max(1, remaining * portions[i] // whole), rest)
            holding[i] = holding[i] + extra
            rest = rest - extra
    return np.array(holding)


def gaussian(stream_key, dims, width, limit, cuts=(), held_as=jnp.bfloat16):
    factor_of = levels(stream_key, dims, cuts, -0.22, 0.18) if cuts else 1.0
    entries = jax.random.normal(stream_key, dims, jnp.float32) * width * factor_of
    return jnp.minimum(jnp.maximum(entries, -limit), limit).astype(held_as)


def setup_inputs(seed: int = 0) -> dict:
    keys = jax.random.split(jax.random.key(seed), 8)
    tokens = gaussian(keys[0], (TOKENS, D), 1.0, 6.0, ((0, 32),))
    route_keys = jax.random.split(jax.random.fold_in(keys[1], 1), TOKENS // TOK_DEV)
    route_turns = jax.random.permutation(jax.random.fold_in(keys[1], 3), TOKENS // TOK_DEV)
    route = jax.vmap(lambda own, number: routed_block(jax.random.fold_in(keys[1], 2), own, number, TOK_DEV, EXPERTS, 1, CAP, 2))(route_keys, route_turns).reshape((TOKENS, 1))
    norm_gain = jnp.clip(1.0 + 0.1 * jax.random.normal(keys[2], (D,), jnp.float32), 0.5, 1.5).astype(jnp.bfloat16)
    router_weight = gaussian(keys[3], (D, EXPERTS), 0.02, 0.119628906)
    w_in = gaussian(keys[4], (EXPERTS, D, FF), D ** -0.5, 0.1875, ((0, 4), (2, 4)))
    w_out = gaussian(keys[5], (EXPERTS, FF, D), 0.15, 0.8984375, ((0, 4), (1, 4)))
    cotangent = gaussian(keys[6], (TOKENS, D), 1.0, 6.0, ((0, 32),))
    return dict(tokens=tokens, route=route, norm_gain=norm_gain, router_weight=router_weight, w_in=w_in, w_out=w_out, cotangent=cotangent)


HIGHEST = lax.Precision.HIGHEST
EPSILON = 1e-05

@jax.custom_vjp
def low(v):
    return lax.optimization_barrier(v.astype(jnp.bfloat16)).astype(jnp.float32)

@jax.custom_vjp
def low_back(v):
    return v

def low_keep(v):
    return (low(v), None)

def low_pass(kept, grad):
    return (grad,)

def back_keep(v):
    return (v, None)

def back_low(kept, grad):
    return (low(grad),)
low.defvjp(low_keep, low_pass)
low_back.defvjp(back_keep, back_low)

def activate(values):
    return jax.nn.gelu(values, approximate=True)

def slot_index(chosen):
    onehot = (chosen[:, None] == jnp.arange(EXPERTS, dtype=jnp.int32)[None, :]).astype(jnp.int32)
    counted = jnp.cumsum(onehot.reshape(TOKENS // TOK_DEV, TOK_DEV, EXPERTS), axis=1).reshape(TOKENS, EXPERTS)
    within = lax.optimization_barrier(jnp.sum((counted - 1) * onehot, axis=1)).astype(jnp.int32)
    blocks = jnp.arange(TOKENS, dtype=jnp.int32) // TOK_DEV
    return (blocks * (EXPERTS * CAP) + chosen * CAP + within).astype(jnp.int32)

def expert_rows(packed):
    rows_in, first_weight, second_weight = packed
    hidden_pre = low_back(jnp.dot(rows_in, first_weight, precision=HIGHEST))
    hidden_low = low(activate(hidden_pre))
    return jnp.dot(hidden_low, second_weight, precision=HIGHEST)

def forward(inputs, gain_f32, router_f32, first_all, second_all, chosen, target):
    inverse = lax.rsqrt(lax.optimization_barrier(jnp.mean(inputs * inputs, axis=1, keepdims=True)) + EPSILON)
    normed_low = low(inputs * inverse * gain_f32[None, :])
    expert_in = low_back(normed_low)
    logits = jnp.dot(normed_low, router_f32, precision=HIGHEST)
    softmax_out = jax.nn.softmax(logits, axis=1)
    onehot = (chosen[:, None] == jnp.arange(EXPERTS, dtype=jnp.int32)[None, :]).astype(inputs.dtype)
    gate_value = lax.optimization_barrier(jnp.sum(softmax_out * onehot, axis=1, keepdims=True))
    block_count = TOKENS // TOK_DEV
    buckets = jnp.zeros((block_count * EXPERTS * CAP, D), inputs.dtype).at[target].set(expert_in)
    buckets = buckets.reshape(block_count, EXPERTS, CAP, D).transpose(1, 0, 2, 3).reshape(EXPERTS, block_count * CAP, D)
    results = lax.map(jax.checkpoint(expert_rows), (buckets, first_all, second_all))
    results = results.reshape(EXPERTS, block_count, CAP, D).transpose(1, 0, 2, 3).reshape(block_count * EXPERTS * CAP, D)
    expert_out = low_back(low(results))[target]
    return inputs + gate_value * expert_out

def reference(tokens, route, norm_gain, router_weight, w_in, w_out, cotangent):
    chosen = route[:, 0].astype(jnp.int32)
    target = slot_index(chosen)
    inputs = tokens.astype(jnp.float32)

    def closed(a_in, b_in, c_in, d_in, e_in):
        return forward(a_in, b_in, c_in, d_in, e_in, chosen, target)
    result, pullback = jax.vjp(closed, inputs, norm_gain.astype(jnp.float32), router_weight.astype(jnp.float32), w_in.astype(jnp.float32), w_out.astype(jnp.float32))
    grads = pullback(cotangent.astype(jnp.float32))
    return (result.astype(jnp.bfloat16), grads[0], grads[1], grads[2], grads[3], grads[4])
```

```python
import functools

import jax
import jax.numpy as jnp
from jax import lax
from jax.experimental import pallas as pl
from jax.experimental.pallas import tpu as pltpu
from jax.sharding import PartitionSpec as P

HIGHEST = lax.Precision.HIGHEST
MESH = pl.DeviceIdType.MESH
EPSILON = 1e-05
F32 = jnp.float32
BF16 = jnp.bfloat16
AXES = ("dp", "expert", "hidden")
C0 = 0.7978845608
C1 = 0.044715


def flip(index, mask):
    out, bit = index, 1
    while bit <= mask:
        if mask & bit:
            out = out + bit - 2 * bit * lax.rem(lax.div(index, bit), 2)
        bit *= 2
    return out


def dot_nn(a, b):
    return lax.dot_general(a, b, (((1,), (0,)), ((), ())), preferred_element_type=F32)


def dot_nt(a, b):
    return lax.dot_general(a, b, (((1,), (1,)), ((), ())), preferred_element_type=F32)


def dot_tn(a, b):
    return lax.dot_general(a, b, (((0,), (0,)), ((), ())), preferred_element_type=F32)


def block_kernel(
    experts, pairs, order, hidden_tile, weight_parts, grad_parts,
    x_ref, route_ref, gain_ref, router_ref, win_ref, wout_ref, cot_ref,
    act_ref, ig_ref, red_ref, ga_in, ga_out, gb_in, gb_out, back_n, back_g,
    normed, place, inv, gate, probs, bn, bg, xs, gs, hs, ps, wp_in, wp_out, y_in, y_out,
    rs_send, rs_n, rs_g, own_n, own_g, total, red_in,
    w_send, w_recv, wf_send, wf_recv, z_send, z_recv, f_send, f_recv, r_send, r_recv,
    b_send, b_recv, y_send, y_recv, d_send, d_recv, red_send, red_recv, local,
):
    tokens, width = x_ref.shape
    hid = win_ref.shape[1]
    cap = bn.shape[0] // experts
    dp, z, h = (lax.axis_index(a) for a in AXES)
    c = lax.rem(h, 2)
    parity = lax.rem(dp, 2)
    core_peer = (dp, z, flip(h, 1))
    y_peer = (dp, z, flip(h, 2))
    x_peer = (flip(dp, 1), z, h)

    def remote(src, dst, send, recv, peer):
        return pltpu.make_async_remote_copy(
            src_ref=src, dst_ref=dst, send_sem=send, recv_sem=recv, device_id=peer, device_id_type=MESH
        )

    dp_steps = [1 << s for s in range(8) if (1 << s) < pairs]
    peers = [core_peer, y_peer] + [(flip(dp, m), z, h) for m in dp_steps]
    peers += [(dp, flip(z, k), h) for k in range(1, experts)]
    barrier = pltpu.get_barrier_semaphore()
    for peer in peers:
        pl.semaphore_signal(barrier, inc=1, device_id=peer, device_id_type=MESH)
    pl.semaphore_wait(barrier, len(peers))

    mats = ((win_ref, wp_in), (wout_ref, wp_out))

    def weight_copy(which, part):
        src, dst = mats[which]
        rows = src.shape[0] // weight_parts
        span = pl.ds(part * rows, rows)
        return remote(src.at[span], dst.at[span], w_send.at[part], w_recv.at[part], y_peer)

    def weight_pass(which, part):
        dst = mats[which][1]
        rows = dst.shape[0] // weight_parts
        span = pl.ds(part * rows, rows)
        return remote(dst.at[span], dst.at[span], wf_send.at[part], wf_recv.at[part], x_peer)

    for which in (0, 1):
        @pl.when(parity == which)
        def _():
            for part in range(weight_parts):
                weight_copy(which, part).start()

    tile = 128
    lane_e = lax.broadcasted_iota(jnp.int32, (tokens, experts), 1)
    onehot = (route_ref[...] == lane_e).astype(BF16)

    @pl.loop(0, tokens // tile)
    def _(i):
        rows = pl.ds(pl.multiple_of(i * tile, tile), tile)
        x = x_ref[rows, :].astype(F32)
        inverse = lax.rsqrt(jnp.mean(x * x, axis=1, keepdims=True) + EPSILON)
        low = (x * inverse * gain_ref[...].astype(F32)).astype(BF16)
        normed[rows, :] = low
        inv[rows, :] = inverse
        logits = dot_nn(low, router_ref[...])
        shifted = jnp.exp(logits - jnp.max(logits, axis=1, keepdims=True))
        soft = shifted / jnp.sum(shifted, axis=1, keepdims=True)
        probs[rows, :] = soft
        chosen = route_ref[rows, :]
        hot = (chosen == lax.broadcasted_iota(jnp.int32, (tile, experts), 1)).astype(F32)
        gate[rows, :] = jnp.sum(soft * hot, axis=1, keepdims=True)
        before = (
            lax.broadcasted_iota(jnp.int32, (tile, tokens), 1)
            < lax.broadcasted_iota(jnp.int32, (tile, tokens), 0) + i * tile
        ).astype(BF16)
        rank = jnp.sum(dot_nn(before, onehot) * hot, axis=1, keepdims=True)
        slot = chosen * cap + rank.astype(jnp.int32)
        place[rows, :] = (
            slot == lax.broadcasted_iota(jnp.int32, (tile, experts * cap), 1)
        ).astype(BF16)

    out_g = (gate[...] * cot_ref[...].astype(F32)).astype(BF16)

    def slots(e):
        return pl.ds(pl.multiple_of(e * cap, cap), cap)

    def arrive(source, core):
        return pl.ds(pl.multiple_of((source * 2 + core) * cap, cap), cap)

    def z_copy(t, k):
        src, dst = ((bn, xs), (bg, gs))[t]
        e = flip(z, k)
        return remote(
            src.at[slots(e)], dst.at[arrive(z, c)], z_send.at[t, k], z_recv.at[t, k], (dp, e, h)
        )

    def pair_copy(t, k):
        buf = (xs, gs)[t]
        span = arrive(flip(z, k), c)
        return remote(buf.at[span], buf.at[span], f_send.at[t, k], f_recv.at[t, k], core_peer)

    for k in order:
        e = flip(z, k)
        pick = place[:, slots(e)]
        if k == 0:
            xs[arrive(z, c), :] = dot_tn(pick, normed[...]).astype(BF16)
            gs[arrive(z, c), :] = dot_tn(pick, out_g).astype(BF16)
            for t in (0, 1):
                pair_copy(t, 0).start()
        else:
            bn[slots(e), :] = dot_tn(pick, normed[...]).astype(BF16)
            z_copy(0, k).start()
            bg[slots(e), :] = dot_tn(pick, out_g).astype(BF16)
            z_copy(1, k).start()

    for which in (0, 1):
        @pl.when(parity == which)
        def _():
            for part in range(weight_parts):
                weight_copy(which, part).wait_recv()
                weight_pass(which, part).start()
            for part in range(weight_parts):
                weight_pass(1 - which, part).wait_recv()

    def rs_copy(t, k, slot):
        dst = (rs_n, rs_g)[t]
        return remote(
            rs_send.at[slot, t], dst.at[pl.ds(k * cap, cap)], r_send.at[t, k], r_recv.at[t, k], core_peer
        )

    def back_copy(t, k):
        src, dst = ((rs_n, back_n), (rs_g, back_g))[t]
        e = flip(z, k)
        return remote(
            src.at[pl.ds(k * cap, cap)], dst.at[slots(z)], b_send.at[t, k], b_recv.at[t, k], (dp, e, h)
        )

    def back_local(t):
        src, dst = ((rs_n, back_n), (rs_g, back_g))[t]
        return pltpu.make_async_copy(src.at[pl.ds(0, cap)], dst.at[slots(z)], local.at[t, 0])

    for turn, k in enumerate(order):
        source = flip(z, k)
        slot = turn % 2
        for t in (0, 1):
            if k:
                z_copy(t, k).wait_recv()
                pair_copy(t, k).start()
        for t in (0, 1):
            pair_copy(t, k).wait_recv()
        chunk = pl.ds(pl.multiple_of(source * 2 * cap, 2 * cap), 2 * cap)
        for half, (first, second) in enumerate(((win_ref, wout_ref), (wp_in, wp_out))):
            @pl.loop(0, hid // hidden_tile)
            def _(j):
                cols = pl.ds(pl.multiple_of(j * hidden_tile, hidden_tile), hidden_tile)
                pre = dot_nn(xs[chunk, :], first[:, cols])
                back = dot_nt(gs[chunk, :], second[cols, :])
                square = pre * pre
                curve = jnp.tanh(C0 * pre * (1.0 + C1 * square))
                low_half = 0.5 * (1.0 + curve)
                slope = low_half + (0.5 * C0) * pre * (1.0 - curve * curve) * (1.0 + (3.0 * C1) * square)
                at = pl.ds(pl.multiple_of(half * hid + j * hidden_tile, hidden_tile), hidden_tile)
                hs[chunk, at] = (pre * low_half).astype(BF16)
                ps[chunk, at] = (back * slope).astype(BF16)

        def partial_n(rows):
            return dot_nn(hs[rows, pl.ds(0, hid)], wout_ref[...]) + dot_nn(hs[rows, pl.ds(hid, hid)], wp_out[...])

        def partial_g(rows):
            return dot_nt(ps[rows, pl.ds(0, hid)], win_ref[...]) + dot_nt(ps[rows, pl.ds(hid, hid)], wp_in[...])

        theirs, ours = arrive(source, 1 - c), arrive(source, c)
        if turn >= 2:
            for t in (0, 1):
                rs_copy(t, order[turn - 2], slot).wait_send()
        rs_send[slot, 0] = partial_n(theirs).astype(BF16)
        rs_copy(0, k, slot).start()
        rs_send[slot, 1] = partial_g(theirs).astype(BF16)
        rs_copy(1, k, slot).start()
        own_n[...] = partial_n(ours)
        own_g[...] = partial_g(ours)
        for t, (own, got) in enumerate(((own_n, rs_n), (own_g, rs_g))):
            rs_copy(t, k, slot).wait_recv()
            span = pl.ds(k * cap, cap)
            got[span, :] = (own[...] + got[span, :].astype(F32)).astype(BF16)
            if k:
                back_copy(t, k).start()
            else:
                back_local(t).start()

    for which in (0, 1):
        @pl.when(parity == which)
        def _():
            for part in range(weight_parts):
                weight_copy(which, part).wait_send()
                weight_pass(which, part).wait_send()

    heights = (width // grad_parts, hid // grad_parts)
    piece = 128

    def span_of(t, i, sub=None):
        if sub is None:
            return pl.ds(pl.multiple_of(i * heights[t], heights[t]), heights[t])
        return pl.ds(pl.multiple_of(i * heights[t] + sub * piece, piece), piece)

    pieces = [(t, sub) for t in (0, 1) for sub in range(heights[t] // piece)]

    def y_copy(t, i, sub):
        src, dst = ((wp_in, y_in), (wp_out, y_out))[t]
        span, at = span_of(t, i, sub), i * (heights[t] // piece) + sub
        return remote(src.at[span], dst.at[span], y_send.at[t, at], y_recv.at[t, at], y_peer)

    def d_copy(t, i, sub):
        src, dst = ((y_in, gb_in), (y_out, gb_out))[t]
        span, at = span_of(t, i, sub), i * (heights[t] // piece) + sub
        return remote(src.at[span], dst.at[span], d_send.at[t, at], d_recv.at[t, at], x_peer)

    def d_local(t, i, sub):
        src, dst = ((y_in, ga_in), (y_out, ga_out))[t]
        span, at = span_of(t, i, sub), i * (heights[t] // piece) + sub
        return pltpu.make_async_copy(src.at[span], dst.at[span], local.at[2 + t, at])

    def weight_grad(t, i, half):
        if t == 0:
            return dot_tn(xs[:, span_of(0, i)], ps[:, pl.ds(half * hid, hid)])
        at = pl.ds(pl.multiple_of(half * hid + i * heights[1], heights[1]), heights[1])
        return dot_tn(hs[:, at], gs[...])

    @pl.loop(0, grad_parts)
    def _(i):
        for t in (0, 1):
            (wp_in, wp_out)[t][span_of(t, i), :] = weight_grad(t, i, 1).astype(BF16)
            for sub in range(heights[t] // piece):
                y_copy(t, i, sub).start()

    @pl.loop(0, grad_parts)
    def _(i):
        for t in (0, 1):
            mine = weight_grad(t, i, 0)
            got = (y_in, y_out)[t]
            for sub in range(heights[t] // piece):
                span = span_of(t, i, sub)
                y_copy(t, i, sub).wait_recv()
                got[span, :] = (mine[sub * piece:(sub + 1) * piece] + got[span, :].astype(F32)).astype(BF16)
                if pairs == 2:
                    d_copy(t, i, sub).start()
                d_local(t, i, sub).start()

    for k in range(1, experts):
        for t in (0, 1):
            z_copy(t, k).wait_send()
            back_copy(t, k).wait_recv()
            back_copy(t, k).wait_send()
    for t in (0, 1):
        back_local(t).wait()
        got = pltpu.make_async_copy((back_n, back_g)[t], (bn, bg)[t], local.at[t, 0])
        got.start()
        got.wait()

    total[...] = jnp.zeros_like(total)

    @pl.loop(0, tokens // tile)
    def _(i):
        rows = pl.ds(pl.multiple_of(i * tile, tile), tile)
        spots = place[rows, :]
        expert_out = dot_nn(spots, bn[...])
        expert_g = dot_nn(spots, bg[...])
        x = x_ref[rows, :].astype(F32)
        up = cot_ref[rows, :].astype(F32)
        g, inverse, soft = gate[rows, :], inv[rows, :], probs[rows, :]
        hot = (route_ref[rows, :] == lax.broadcasted_iota(jnp.int32, (tile, experts), 1)).astype(F32)
        act_ref[rows, :] = (x + g * expert_out).astype(BF16)
        gate_g = jnp.sum(up * expert_out, axis=1, keepdims=True)
        logit_g = gate_g * g * (hot - soft)
        low = normed[rows, :].astype(F32)
        total[pl.ds(0, experts), :] += lax.dot_general(
            logit_g, low, (((0,), (0,)), ((), ())), precision=HIGHEST, preferred_element_type=F32
        )
        normed_router = lax.dot_general(
            logit_g, router_ref[...].astype(F32), (((1,), (1,)), ((), ())),
            precision=HIGHEST, preferred_element_type=F32,
        )
        normed_g = expert_g + normed_router
        total[pl.ds(experts, 1), :] += jnp.sum(normed_g * x * inverse, axis=0, keepdims=True)
        u = gain_ref[...].astype(F32) * normed_g
        dot = jnp.sum(u * x, axis=1, keepdims=True)
        ig_ref[rows, :] = up + inverse * u - x * (inverse * inverse * inverse * dot / width)

    steps = [core_peer, y_peer] + [(flip(dp, m), z, h) for m in dp_steps]
    steps += [(dp, flip(z, m), h) for m in [1 << s for s in range(8)] if m < experts]
    for s, peer in enumerate(steps):
        copy = remote(total, red_in.at[s], red_send.at[s], red_recv.at[s], peer)
        copy.start()
        copy.wait()
        total[...] += red_in[s]
    red_ref[...] = total[...]

    for k in range(experts):
        for t in (0, 1):
            pair_copy(t, k).wait_send()
    for turn in range(max(0, experts - 2), experts):
        for t in (0, 1):
            rs_copy(t, order[turn], turn % 2).wait_send()

    @pl.loop(0, grad_parts)
    def _(i):
        for t, sub in pieces:
            y_copy(t, i, sub).wait_send()
            d_local(t, i, sub).wait()
            if pairs == 2:
                d_copy(t, i, sub).wait()


def on_device(tokens, route, norm_gain, router_weight, w_in, w_out, cotangent):
    rows, width = tokens.shape
    experts = lax.axis_size("expert")
    pairs = lax.axis_size("dp")
    cap = 2 * rows // experts
    hid = w_in.shape[2]
    order = [0, 2, 3, 1] + list(range(4, experts))
    order = [k for k in order if k < experts]
    hidden_tile = 256
    weight_parts, grad_parts = 4, 3
    grad_pieces = max(width, hid) // 128
    slot_rows = experts * cap
    both = 2 * slot_rows
    red_rows = 8 * ((experts + 1 + 7) // 8)
    reduce_steps = 2 + (pairs - 1).bit_length() + (experts - 1).bit_length()
    vmem = pl.BlockSpec(memory_space=pltpu.VMEM)
    hbm = pl.BlockSpec(memory_space=pl.ANY)
    sem = pltpu.SemaphoreType.DMA
    shape = jax.ShapeDtypeStruct
    out = pl.pallas_call(
        functools.partial(block_kernel, experts, pairs, order, hidden_tile, weight_parts, grad_parts),
        out_shape=[
            shape((rows, width), BF16),
            shape((rows, width), F32),
            shape((red_rows, width), F32),
            shape((width, hid), BF16),
            shape((hid, width), BF16),
            shape((width, hid), BF16),
            shape((hid, width), BF16),
            shape((slot_rows, width), BF16),
            shape((slot_rows, width), BF16),
        ],
        in_specs=[vmem] * 7,
        out_specs=[vmem] * 3 + [hbm] * 6,
        scratch_shapes=[
            pltpu.VMEM((rows, width), BF16),
            pltpu.VMEM((rows, slot_rows), BF16),
            pltpu.VMEM((rows, 1), F32),
            pltpu.VMEM((rows, 1), F32),
            pltpu.VMEM((rows, experts), F32),
            pltpu.VMEM((slot_rows, width), BF16),
            pltpu.VMEM((slot_rows, width), BF16),
            pltpu.VMEM((both, width), BF16),
            pltpu.VMEM((both, width), BF16),
            pltpu.VMEM((both, 2 * hid), BF16),
            pltpu.VMEM((both, 2 * hid), BF16),
            pltpu.VMEM((width, hid), BF16),
            pltpu.VMEM((hid, width), BF16),
            pltpu.VMEM((width, hid), BF16),
            pltpu.VMEM((hid, width), BF16),
            pltpu.VMEM((2, 2, cap, width), BF16),
            pltpu.VMEM((slot_rows, width), BF16),
            pltpu.VMEM((slot_rows, width), BF16),
            pltpu.VMEM((cap, width), F32),
            pltpu.VMEM((cap, width), F32),
            pltpu.VMEM((red_rows, width), F32),
            pltpu.VMEM((reduce_steps, red_rows, width), F32),
            sem((weight_parts,)), sem((weight_parts,)), sem((weight_parts,)), sem((weight_parts,)),
            sem((2, experts)), sem((2, experts)), sem((2, experts)), sem((2, experts)),
            sem((2, experts)), sem((2, experts)), sem((2, experts)), sem((2, experts)),
            sem((2, grad_pieces)), sem((2, grad_pieces)), sem((2, grad_pieces)), sem((2, grad_pieces)),
            sem((reduce_steps,)), sem((reduce_steps,)), sem((4, grad_pieces)),
        ],
        compiler_params=pltpu.CompilerParams(
            collective_id=0, has_side_effects=True, vmem_limit_bytes=62 * 1024 * 1024
        ),
    )(tokens, route, norm_gain[None, :], router_weight, w_in[0], w_out[0], cotangent)
    activations, input_grad, red, ga_in, ga_out, gb_in, gb_out = out[:7]
    if pairs == 2:
        first_grad = ga_in.astype(F32) + gb_in.astype(F32)
        second_grad = ga_out.astype(F32) + gb_out.astype(F32)
    else:
        first_grad, second_grad = lax.psum((ga_in.astype(F32), ga_out.astype(F32)), "dp")
    return (
        activations, input_grad, red[experts], red[:experts].T, first_grad[None], second_grad[None],
    )


def solution(mesh):
    placed = (
        P(AXES, None),
        P(AXES, None),
        P(),
        P(),
        P("expert", None, "hidden"),
        P("expert", "hidden", None),
        P(AXES, None),
    )
    return jax.shard_map(
        on_device,
        mesh=mesh,
        in_specs=placed,
        out_specs=(
            P(AXES, None),
            P(AXES, None),
            P(),
            P(),
            P("expert", None, "hidden"),
            P("expert", "hidden", None),
        ),
        check_vma=False,
    )
```

```python
import functools

import jax
import jax.numpy as jnp
from jax import lax
from jax.experimental import pallas as pl
from jax.experimental.pallas import tpu as pltpu
from jax.sharding import PartitionSpec as P

HIGHEST = lax.Precision.HIGHEST
MESH = pl.DeviceIdType.MESH
EPSILON = 1e-05
F32 = jnp.float32
BF16 = jnp.bfloat16
AXES = ("dp", "expert", "hidden")
C0 = 0.7978845608
C1 = 0.044715
TILE = 128
PIECE = 128
SMALL = 64


def flip(index, mask, limit):
    out, bit = 0, 1
    while bit < limit:
        a, b = lax.rem(lax.div(index, bit), 2), lax.rem(lax.div(mask, bit), 2)
        out = out + bit * (a + b - 2 * a * b)
        bit *= 2
    return out


def contract(a, b, left, right, **kwargs):
    return lax.dot_general(a, b, (((left,), (right,)), ((), ())), preferred_element_type=F32, **kwargs)


def dot_nn(a, b):
    return contract(a, b, 1, 0)


def dot_nt(a, b):
    return contract(a, b, 1, 1)


def dot_tn(a, b):
    return contract(a, b, 0, 0)


def remote(src, dst, send, recv, peer):
    return pltpu.make_async_remote_copy(
        src_ref=src, dst_ref=dst, send_sem=send, recv_sem=recv, device_id=peer, device_id_type=MESH
    )


def plane_peer(i, pairs, halves):
    dp, z, h = (lax.axis_index(a) for a in AXES)
    return lax.rem(dp + lax.div(i, halves), pairs), z, lax.rem(h + lax.rem(i, halves), halves)


def line_peer(i, experts):
    dp, z, h = (lax.axis_index(a) for a in AXES)
    return dp, lax.rem(z + i, experts), h


def signal_all(pairs, experts, halves):
    barrier = pltpu.get_barrier_semaphore()

    @pl.loop(1, pairs * halves)
    def _(i):
        pl.semaphore_signal(barrier, inc=1, device_id=plane_peer(i, pairs, halves), device_id_type=MESH)

    @pl.loop(1, experts)
    def _(i):
        pl.semaphore_signal(barrier, inc=1, device_id=line_peer(i, experts), device_id_type=MESH)


def wait_all(pairs, experts, halves):
    pl.semaphore_wait(pltpu.get_barrier_semaphore(), pairs * halves + experts - 2)


def prologue_kernel(
    experts, pairs, halves, cold,
    x_hbm, route_ref, gain_ref, router_ref, cot_hbm,
    bn_out, bg_out, aux_ref, level_ref,
    x_ref, cot_ref, place, router, ranks, stage, counts, count_in, line_in, send, recv, load, local,
):
    tokens, width = x_ref.shape
    cap = bn_out.shape[0] // experts
    signal_all(pairs, experts, halves)
    loads = [
        pltpu.make_async_copy(src, dst, load.at[i])
        for i, (src, dst) in enumerate(((x_hbm, x_ref), (cot_hbm, cot_ref)))
    ]
    for copy in loads:
        copy.start()

    lane = lax.broadcasted_iota(jnp.int32, (tokens, TILE), 1)
    chosen = jnp.transpose(jnp.broadcast_to(route_ref[...].astype(F32), (TILE, tokens)))
    onehot = (chosen.astype(jnp.int32) == lane).astype(F32)
    counts[...] = jnp.broadcast_to(jnp.sum(onehot, axis=0, keepdims=True), (8, TILE))
    before = (
        lax.broadcasted_iota(jnp.int32, (tokens, tokens), 1) < lax.broadcasted_iota(jnp.int32, (tokens, tokens), 0)
    ).astype(BF16)
    rank = jnp.sum(dot_nn(before, onehot.astype(BF16)) * onehot, axis=1, keepdims=True)
    ranks[0] = chosen
    ranks[1] = chosen * cap + rank
    router[...] = jnp.zeros_like(router)
    router[pl.ds(0, experts), :] = router_ref[...]

    here = pairs * halves

    def plane_copy(i):
        return remote(counts, count_in.at[i], send.at[i], recv.at[i], plane_peer(i, pairs, halves))

    def line_copy(i):
        at = here - 1 + i
        return remote(count_in.at[0], line_in.at[i], send.at[at], recv.at[at], line_peer(i, experts))

    wait_all(pairs, experts, halves)

    @pl.loop(1, here)
    def _(i):
        plane_copy(i).start()

    for copy in loads:
        copy.wait()

    @pl.loop(0, tokens // TILE)
    def _(i):
        rows = pl.ds(pl.multiple_of(i * TILE, TILE), TILE)
        x = x_ref[rows, :].astype(F32)
        inverse = lax.rsqrt(jnp.mean(x * x, axis=1, keepdims=True) + EPSILON)
        low = (x * inverse * gain_ref[...].astype(F32)).astype(BF16)
        x_ref[rows, :] = low
        lanes = lax.broadcasted_iota(jnp.int32, (TILE, TILE), 1)
        expert, slot = ranks[0, rows, :], ranks[1, rows, :]
        logits = jnp.where(lanes < experts, dot_nt(low, router[...]), -jnp.inf)
        shifted = jnp.exp(logits - jnp.max(logits, axis=1, keepdims=True))
        soft = shifted / jnp.sum(shifted, axis=1, keepdims=True)
        gate = jnp.sum(jnp.where(expert.astype(jnp.int32) == lanes, soft, 0.0), axis=1, keepdims=True)
        cot_ref[rows, :] = (gate * cot_ref[rows, :].astype(F32)).astype(BF16)
        aux = jnp.where(lanes == experts, gate, soft)
        aux = jnp.where(lanes == experts + 1, inverse, aux)
        aux = jnp.where(lanes == experts + 2, slot, aux)
        aux_ref[rows, :] = jnp.where(lanes == experts + 3, expert, aux)
        slot_int = slot.astype(jnp.int32)
        for j in range(experts * cap // TILE):
            place[rows, pl.ds(j * TILE, TILE)] = (slot_int == lanes + j * TILE).astype(BF16)

    most = counts[...]
    for i in range(1, here):
        plane_copy(i).wait_recv()
        most = jnp.maximum(most, count_in[i])
    count_in[0] = most

    @pl.loop(1, experts)
    def _(i):
        line_copy(i).start()

    def out_copy(t, e):
        span = pl.ds(pl.multiple_of(e * cap, cap), cap)
        return pltpu.make_async_copy(stage.at[t, span], (bn_out, bg_out)[t].at[span], local.at[t, e])

    @pl.loop(0, experts)
    def _(e):
        span = pl.ds(pl.multiple_of(e * cap, cap), cap)
        for t, values in enumerate((x_ref, cot_ref)):
            stage[t, span, :] = dot_tn(place[:, span], values[...]).astype(BF16)
            out_copy(t, e).start()

    most = count_in[0]
    for i in range(1, experts):
        line_copy(i).wait_recv()
        most = jnp.maximum(most, line_in[i])
    lanes = lax.broadcasted_iota(jnp.int32, (8, TILE), 1)
    rows = lax.broadcasted_iota(jnp.int32, (8, TILE), 0)
    over = jnp.where((most > cold) & (rows == 0), 1.0, 0.0)
    crowded = jnp.sum(over)
    which = jnp.sum(over * lanes.astype(F32))
    level_ref[0] = jnp.where(crowded <= 1.0, which, float(experts)).astype(jnp.int32)

    @pl.loop(1, here)
    def _(i):
        plane_copy(i).wait_send()

    @pl.loop(1, experts)
    def _(i):
        line_copy(i).wait_send()

    @pl.loop(0, experts)
    def _(e):
        for t in (0, 1):
            out_copy(t, e).wait()


def block_kernel(
    experts, pairs, halves, hot, cold, hidden_tile, weight_parts, grad_parts,
    x_hbm, aux_hbm, gain_ref, router_ref, win_hbm, wout_hbm, cot_hbm, bn, bg,
    act_hbm, ig_hbm, red_ref, ga_in, ga_out, gb_in, gb_out,
    x_ref, cot_ref, aux_ref, w_in, w_out, act_ref, ig_ref,
    xs, gs, hs, ps, g_in, g_out, y_in, y_out,
    rs_send, rs_n, rs_g, acc_n, acc_g, acc_in, logits, ret_n, ret_g, total, red_plane, red_line,
    w_send, w_recv, wf_send, wf_recv, z_send, z_recv, f_send, f_recv, r_send, r_recv,
    b_send, b_recv, y_send, y_recv, d_send, d_recv, red_send, red_recv, load, local, out_sem, all_in,
):
    tokens, width = x_ref.shape
    hid = w_in.shape[2]
    cap = bn.shape[0] // experts
    dp, z, h = (lax.axis_index(a) for a in AXES)
    c = lax.rem(h, 2)
    parity = lax.rem(dp, 2)
    core_peer = (dp, z, flip(h, 1, halves))
    y_peer = (dp, z, flip(h, 2, halves))
    x_peer = (flip(dp, 1, pairs), z, h)
    here = pairs * halves
    signal_all(pairs, experts, halves)
    wait_all(pairs, experts, halves)

    def sized(e, act):
        if hot is None:
            act(cap)
        else:
            @pl.when(e == hot)
            def _():
                act(cap)

            @pl.when(e != hot)
            def _():
                act(cold)

    def slots(e, rows=cap):
        return pl.ds(pl.multiple_of(e * cap, cap), rows)

    def arrive(source, core, rows=cap):
        return pl.ds(pl.multiple_of((source * 2 + core) * cap, cap), rows)

    def turn_k(turn):
        return flip(turn, lax.div(turn, 2), experts)

    def z_copy(t, k, rows):
        src, dst = ((bn, xs), (bg, gs))[t]
        e = flip(z, k, experts)
        return remote(
            src.at[slots(e, rows)], dst.at[arrive(z, c, rows)], z_send.at[t, k], z_recv.at[t, k], (dp, e, h)
        )

    def z_start(t, k):
        sized(flip(z, k, experts), lambda rows: z_copy(t, k, rows).start())

    early = max(1, experts - 1)

    @pl.loop(1, early)
    def _(n):
        for t in (0, 1):
            z_start(t, turn_k(early - n))

    mats = ((win_hbm, w_in), (wout_hbm, w_out))

    def weight_copy(which, part):
        src, dst = mats[which]
        rows = src.shape[0] // weight_parts
        span = pl.ds(pl.multiple_of(part * rows, rows), rows)
        return remote(src.at[span], dst.at[1, span], w_send.at[part], w_recv.at[part], y_peer)

    def weight_pass(which, part):
        dst = mats[which][1]
        rows = dst.shape[1] // weight_parts
        span = pl.ds(pl.multiple_of(part * rows, rows), rows)
        return remote(dst.at[1, span], dst.at[1, span], wf_send.at[part], wf_recv.at[part], x_peer)

    for which in (0, 1):
        @pl.when(parity == which)
        def _():
            @pl.loop(0, weight_parts)
            def _(part):
                weight_copy(which, part).start()

    def pair_copy(t, k, rows):
        buf = (xs, gs)[t]
        span = arrive(flip(z, k, experts), c, rows)
        return remote(buf.at[span], buf.at[span], f_send.at[t, k], f_recv.at[t, k], core_peer)

    def own_pair(t, rows):
        src, dst = ((bn, xs), (bg, gs))[t]
        return remote(
            src.at[slots(z, rows)], dst.at[arrive(z, c, rows)], f_send.at[t, 0], f_recv.at[t, 0], core_peer
        )

    def own_local(t, rows):
        src, dst = ((bn, xs), (bg, gs))[t]
        return pltpu.make_async_copy(src.at[slots(z, rows)], dst.at[arrive(z, c, rows)], load.at[t])

    for t in (0, 1):
        sized(z, lambda rows: own_pair(t, rows).start())
        sized(z, lambda rows: own_local(t, rows).start())
    loads = [
        pltpu.make_async_copy(src, dst, load.at[2 + i])
        for i, (src, dst) in enumerate(
            (
                (win_hbm, w_in.at[0]), (wout_hbm, w_out.at[0]),
                (x_hbm, x_ref), (cot_hbm, cot_ref), (aux_hbm, aux_ref),
            )
        )
    ]
    for copy in loads:
        copy.start()

    if hot is not None:
        @pl.when(z != hot)
        def _():
            @pl.loop(0, 2 * experts)
            def _(i):
                rest = pl.ds(pl.multiple_of(i * cap, cap) + cold, cap - cold)
                xs[rest, :] = jnp.zeros((cap - cold, width), BF16)
                gs[rest, :] = jnp.zeros((cap - cold, width), BF16)

        @pl.loop(0, experts)
        def _(e):
            @pl.when(e != hot)
            def _():
                rest = pl.ds(pl.multiple_of(e * cap, cap) + cold, cap - cold)
                ret_n[rest, :] = jnp.zeros((cap - cold, width), BF16)
                ret_g[rest, :] = jnp.zeros((cap - cold, width), BF16)

    for copy in loads:
        copy.wait()
    for t in (0, 1):
        sized(z, lambda rows: own_local(t, rows).wait())

    for which in (0, 1):
        @pl.when(parity == which)
        def _():
            @pl.loop(0, weight_parts)
            def _(part):
                weight_copy(which, part).wait_recv()
                weight_pass(which, part).start()

    final = turn_k(experts - 1)
    if experts > 1:
        for t in (0, 1):
            if experts > 2:
                k = turn_k(experts - 2)
                sized(flip(z, k, experts), lambda rows: z_copy(t, k, rows).wait_send())
            z_start(t, final)

    for which in (0, 1):
        @pl.when(parity == which)
        def _():
            @pl.loop(0, weight_parts)
            def _(part):
                weight_pass(1 - which, part).wait_recv()
                weight_copy(which, part).wait_send()
                weight_pass(which, part).wait_send()

    def token_block(turn):
        k = turn_k(turn)
        source = flip(z, k, experts)

        @pl.when(turn > 0)
        def _():
            for t in (0, 1):
                sized(z, lambda rows: z_copy(t, k, rows).wait_recv())
                sized(z, lambda rows: pair_copy(t, k, rows).start())

        @pl.when(turn == experts - 1)
        def _():
            @pl.loop(1, experts)
            def _(i):
                pl.semaphore_signal(all_in, inc=1, device_id=line_peer(i, experts), device_id_type=MESH)

        for t in (0, 1):
            sized(z, lambda rows: pair_copy(t, k, rows).wait_recv())
        chunk = pl.ds(pl.multiple_of(source * 2 * cap, 2 * cap), 2 * cap)
        per_half = hid // hidden_tile

        @pl.loop(0, 2 * per_half)
        def _(j):
            half = lax.div(j, per_half)
            cols = pl.ds(pl.multiple_of(lax.rem(j, per_half) * hidden_tile, hidden_tile), hidden_tile)
            pre = dot_nn(xs[chunk, :], w_in[half, :, cols])
            back = dot_nt(gs[chunk, :], w_out[half, cols, :])
            square = pre * pre
            curve = jnp.tanh(C0 * pre * (1.0 + C1 * square))
            low_half = 0.5 * (1.0 + curve)
            slope = low_half + (0.5 * C0) * pre * (1.0 - curve * curve) * (1.0 + (3.0 * C1) * square)
            at = pl.ds(pl.multiple_of(j * hidden_tile, hidden_tile), hidden_tile)
            hs[chunk, at] = (pre * low_half).astype(BF16)
            ps[chunk, at] = (back * slope).astype(BF16)

            @pl.when((turn == experts - 1) & (j == 1))
            def _():
                pl.semaphore_wait(all_in, experts - 1)

                @pl.loop(1, experts - 1)
                def _(earlier):
                    held(earlier)

    def rs_copy(t, k, slot):
        return remote(
            rs_send.at[slot, t], (rs_n, rs_g)[t].at[slots(k)], r_send.at[t, k], r_recv.at[t, k], core_peer
        )

    def back_copy(t, k, rows):
        src, dst = ((rs_n, ret_n), (rs_g, ret_g))[t]
        return remote(
            src.at[slots(k, rows)], dst.at[slots(z, rows)], b_send.at[t, k], b_recv.at[t, k],
            (dp, flip(z, k, experts), h),
        )

    def back_start(turn):
        k = turn_k(turn)
        for t in (0, 1):
            sized(z, lambda rows: back_copy(t, k, rows).start())

    def held(turn):
        if hot is None:
            back_start(turn)
        else:
            @pl.when(z != hot)
            def _():
                back_start(turn)

    def token_sums(turn):
        k = turn_k(turn)
        source = flip(z, k, experts)
        slot = lax.rem(turn, 2)

        @pl.when(turn >= 2)
        def _():
            for t in (0, 1):
                rs_copy(t, turn_k(turn - 2), slot).wait_send()

        @pl.loop(0, 2)
        def _(mine):
            rows = arrive(source, lax.rem(1 + c + mine, 2))
            for t, (values, weights, dot, acc) in enumerate(
                ((hs, w_out, dot_nn, acc_n), (ps, w_in, dot_nt, acc_g))
            ):
                acc = acc.at[pl.ds(0, cap)]
                acc[...] = dot(values[rows, pl.ds(0, hid)], weights[0])
                acc[...] += dot(values[rows, pl.ds(hid, hid)], weights[1])

                @pl.when(mine == 0)
                def _():
                    rs_send[slot, t] = acc[...].astype(BF16)
                    rs_copy(t, k, slot).start()

        for t, (acc, got, home) in enumerate(((acc_n, rs_n, ret_n), (acc_g, rs_g, ret_g))):
            rs_copy(t, k, slot).wait_recv()
            both = (acc[pl.ds(0, cap), :] + got[slots(k), :].astype(F32)).astype(BF16)

            @pl.when(turn == 0)
            def _():
                home[slots(z), :] = both

            @pl.when(turn > 0)
            def _():
                got[slots(k), :] = both

    heights = (width // grad_parts, hid // grad_parts)
    subs = tuple(height // PIECE for height in heights)

    def grad_span(t, i, sub=None):
        if sub is None:
            return pl.ds(pl.multiple_of(i * heights[t], heights[t]), heights[t])
        return pl.ds(pl.multiple_of(i * heights[t] + sub * PIECE, PIECE), PIECE)

    def y_copy(t, i, sub):
        src, dst = ((g_in, y_in), (g_out, y_out))[t]
        span, at = grad_span(t, i, sub), i * subs[t] + sub
        return remote(src.at[span], dst.at[span], y_send.at[t, at], y_recv.at[t, at], y_peer)

    def d_copy(t, i, sub):
        src, dst = ((y_in, gb_in), (y_out, gb_out))[t]
        span, at = grad_span(t, i, sub), i * subs[t] + sub
        return remote(src.at[span], dst.at[span], d_send.at[t, at], d_recv.at[t, at], x_peer)

    def d_local(t, i, sub):
        src, dst = ((y_in, ga_in), (y_out, ga_out))[t]
        span, at = grad_span(t, i, sub), i * subs[t] + sub
        return pltpu.make_async_copy(src.at[span], dst.at[span], local.at[t, at])

    accs = (acc_in, acc_n)

    def weight_grad(t, i, half):
        accs[t][...] = jnp.zeros_like(accs[t])
        depth = 2 * cap
        at = pl.ds(pl.multiple_of(half * hid, hid), hid)
        if t:
            at = pl.ds(pl.multiple_of(half * hid + i * heights[1], heights[1]), heights[1])

        @pl.loop(0, experts)
        def _(n):
            rows = pl.ds(pl.multiple_of(n * depth, depth), depth)
            if t == 0:
                accs[t][...] += dot_tn(xs[rows, grad_span(0, i)], ps[rows, at])
            else:
                accs[t][...] += dot_tn(hs[rows, at], gs[rows, :])

    place = hs.at[pl.ds(0, tokens), pl.ds(0, experts * cap)]
    got_n = ps.at[pl.ds(0, tokens), pl.ds(0, width)]
    got_g = ps.at[pl.ds(tokens, tokens), pl.ds(0, width)]
    normed = hs.at[pl.ds(tokens, tokens), pl.ds(0, width)]

    def unbucket():
        @pl.loop(0, tokens // TILE)
        def _(i):
            rows = pl.ds(pl.multiple_of(i * TILE, TILE), TILE)
            slot = aux_ref[rows, experts + 2:experts + 3].astype(jnp.int32)
            lanes = lax.broadcasted_iota(jnp.int32, (TILE, experts * cap), 1)
            place[rows, :] = (slot == lanes).astype(BF16)

        @pl.loop(0, 3)
        def _(n):
            cols = pl.ds(pl.multiple_of(n * (width // 3), width // 3), width // 3)
            got_n[:, cols] = dot_nn(place[...], ret_n[:, cols]).astype(BF16)
            got_g[:, cols] = dot_nn(place[...], ret_g[:, cols]).astype(BF16)

    def out_copy(t, i):
        rows = pl.ds(pl.multiple_of(i * SMALL, SMALL), SMALL)
        src, dst = ((act_ref, act_hbm), (ig_ref, ig_hbm))[t]
        return pltpu.make_async_copy(src.at[rows], dst.at[rows], out_sem.at[t, i])

    def tokens_tile(i):
        rows = pl.ds(pl.multiple_of(i * SMALL, SMALL), SMALL)
        aux = aux_ref[rows, :]
        soft, g, inverse = aux[:, :experts], aux[:, experts:experts + 1], aux[:, experts + 1:experts + 2]
        chosen = aux[:, experts + 3:experts + 4].astype(jnp.int32)
        expert_out = got_n[rows, :].astype(F32)
        expert_g = got_g[rows, :].astype(F32)
        x = x_ref[rows, :].astype(F32)
        up = cot_ref[rows, :].astype(F32)
        gain = gain_ref[...].astype(F32)
        hits = (chosen == lax.broadcasted_iota(jnp.int32, (SMALL, experts), 1)).astype(F32)
        act_ref[rows, :] = (x + g * expert_out).astype(BF16)
        out_copy(0, i).start()
        gate_g = jnp.sum(up * expert_out, axis=1, keepdims=True)
        logit_g = gate_g * g * (hits - soft)
        logits[rows, :] = logit_g
        normed[rows, :] = (x * inverse * gain).astype(BF16)
        normed_g = expert_g
        for e in range(experts):
            normed_g = normed_g + logit_g[:, e:e + 1] * router_ref[e:e + 1, :].astype(F32)
        total[pl.ds(experts, 1), :] += jnp.sum(normed_g * x * inverse, axis=0, keepdims=True)
        u = gain * normed_g
        dot = jnp.sum(u * x, axis=1, keepdims=True)
        ig_ref[rows, :] = up + inverse * u - x * (inverse * inverse * inverse * dot / width)
        out_copy(1, i).start()

    def router_sum():
        rest = logits[...]
        added = jnp.zeros((experts, width), F32)
        for _ in range(3):
            term = rest.astype(BF16)
            added = added + dot_tn(term, normed[...])
            rest = rest - term.astype(F32)
        total[pl.ds(0, experts), :] = added

    def returned():
        @pl.loop(1, experts)
        def _(turn):
            k = turn_k(turn)
            for t in (0, 1):
                sized(flip(z, k, experts), lambda rows: back_copy(t, k, rows).wait_recv())

    def red_plane_copy(i):
        peer = plane_peer(i, pairs, halves)
        return remote(total, red_plane.at[dp * halves + h], red_send.at[i], red_recv.at[i], peer)

    def red_line_copy(i):
        at = here - 1 + i
        return remote(total, red_line.at[z], red_send.at[at], red_recv.at[at], line_peer(i, experts))

    def token_results():
        returned()
        unbucket()
        total[...] = jnp.zeros_like(total)

        @pl.loop(0, tokens // SMALL)
        def _(i):
            tokens_tile(i)

        router_sum()
        red_plane[dp * halves + h] = total[...]

        @pl.loop(1, here)
        def _(i):
            red_plane_copy(i).start()

    def plane_sum():
        @pl.loop(1, here)
        def _(i):
            red_plane_copy(i).wait()

        added = red_plane[0]
        for i in range(1, here):
            added = added + red_plane[i]
        total[...] = added
        red_line[z] = added

        @pl.loop(1, experts)
        def _(i):
            red_line_copy(i).start()

    def grad_step(step):
        half = jnp.where(step < grad_parts, 1, 0)
        i = lax.rem(step, grad_parts)
        for t in (0, 1):
            weight_grad(t, i, half)
            out, got = ((g_in, y_in), (g_out, y_out))[t]

            @pl.when(half == 1)
            def _():
                out[grad_span(t, i), :] = accs[t][...].astype(BF16)

                @pl.loop(0, subs[t])
                def _(sub):
                    y_copy(t, i, sub).start()

            if t:
                @pl.when(step == 2 * grad_parts - 1)
                def _():
                    token_results()

            @pl.when(half == 0)
            def _():
                @pl.loop(0, subs[t])
                def _(sub):
                    span = grad_span(t, i, sub)
                    y_copy(t, i, sub).wait_recv()
                    mine = accs[t][pl.ds(pl.multiple_of(sub * PIECE, PIECE), PIECE), :]
                    got[span, :] = (mine + got[span, :].astype(F32)).astype(BF16)
                    if pairs == 2:
                        d_copy(t, i, sub).start()
                    d_local(t, i, sub).start()

    @pl.loop(0, experts + 2 * grad_parts)
    def _(step):
        late = experts + 1

        @pl.when(((step > 0) & (step < experts)) | (step == late))
        def _():
            token_sums(jnp.where(step < experts, step, experts) - 1)

        @pl.when(step == late)
        def _():
            back_start(experts - 1)

        if hot is not None:
            @pl.when((step > 1) & (step < experts) & (z == hot))
            def _():
                back_start(step - 1)

        @pl.when(step < experts)
        def _():
            token_block(step)

        @pl.when(step >= experts)
        def _():
            grad_step(step - experts)

    plane_sum()

    @pl.loop(1, experts)
    def _(i):
        red_line_copy(i).wait()

    added = red_line[0]
    for i in range(1, experts):
        added = added + red_line[i]
    red_ref[...] = added

    @pl.loop(1, experts)
    def _(turn):
        k = turn_k(turn)
        for t in (0, 1):
            if experts > 2:
                @pl.when(turn != experts - 2)
                def _():
                    sized(flip(z, k, experts), lambda rows: z_copy(t, k, rows).wait_send())
            else:
                sized(flip(z, k, experts), lambda rows: z_copy(t, k, rows).wait_send())
            sized(z, lambda rows: pair_copy(t, k, rows).wait_send())
            sized(z, lambda rows: back_copy(t, k, rows).wait_send())
    for t in (0, 1):
        sized(z, lambda rows: own_pair(t, rows).wait_send())
        for turn in range(max(0, experts - 2), experts):
            rs_copy(t, turn_k(turn), turn % 2).wait_send()

    @pl.loop(0, tokens // SMALL)
    def _(i):
        for t in (0, 1):
            out_copy(t, i).wait()

    @pl.loop(0, grad_parts)
    def _(i):
        for t in (0, 1):
            @pl.loop(0, subs[t])
            def _(sub):
                y_copy(t, i, sub).wait_send()
                d_local(t, i, sub).wait()
                if pairs == 2:
                    d_copy(t, i, sub).wait()


def finish_kernel(experts, act, ig, red, ai, ao, bi, bo, act_out, ig_out, gain_out, router_out, first_out, second_out):
    act_out[...] = act[...]
    ig_out[...] = ig[...]
    first_out[...] = ai[...].astype(F32) + bi[...].astype(F32)
    second_out[...] = ao[...].astype(F32) + bo[...].astype(F32)

    @pl.when(pl.program_id(0) == 0)
    def _():
        gain_out[...] = red[pl.ds(experts, 1), :]
        router_out[...] = red[pl.ds(0, experts), :]


def on_device(tokens, route, norm_gain, router_weight, w_in, w_out, cotangent):
    rows, width = tokens.shape
    experts = lax.axis_size("expert")
    pairs = lax.axis_size("dp")
    halves = lax.axis_size("hidden")
    cap = 2 * rows // experts
    hid = w_in.shape[2]
    cold = 16 * (-(-11 * cap // 256))
    hidden_tile = 256
    weight_parts, grad_parts = 4, 3
    grad_pieces = max(width, hid) // PIECE
    slot_rows = experts * cap
    both = 2 * slot_rows
    red_rows = 8 * ((experts + 1 + 7) // 8)
    peers = pairs * halves + experts
    vmem = pl.BlockSpec(memory_space=pltpu.VMEM)
    hbm = pl.BlockSpec(memory_space=pl.ANY)
    sem = pltpu.SemaphoreType.DMA
    shape = jax.ShapeDtypeStruct
    params = functools.partial(pltpu.CompilerParams, has_side_effects=True, vmem_limit_bytes=62 * 1024 * 1024)
    gain_row = norm_gain[None, :]
    router_rows = router_weight.T

    bn, bg, aux, level = pl.pallas_call(
        functools.partial(prologue_kernel, experts, pairs, halves, cold),
        out_shape=[
            shape((slot_rows, width), BF16),
            shape((slot_rows, width), BF16),
            shape((rows, TILE), F32),
            shape((1,), jnp.int32),
        ],
        in_specs=[hbm, vmem, vmem, vmem, hbm],
        out_specs=[hbm, hbm, vmem, pl.BlockSpec(memory_space=pltpu.SMEM)],
        scratch_shapes=[
            pltpu.VMEM((rows, width), BF16),
            pltpu.VMEM((rows, width), BF16),
            pltpu.VMEM((rows, slot_rows), BF16),
            pltpu.VMEM((TILE, width), BF16),
            pltpu.VMEM((2, rows, TILE), F32),
            pltpu.VMEM((2, slot_rows, width), BF16),
            pltpu.VMEM((8, TILE), F32),
            pltpu.VMEM((pairs * halves, 8, TILE), F32),
            pltpu.VMEM((experts, 8, TILE), F32),
            sem((peers,)), sem((peers,)), sem((2,)), sem((2, experts)),
        ],
        compiler_params=params(collective_id=0),
    )(tokens, route.T, gain_row, router_rows, cotangent)

    def block(hot):
        return pl.pallas_call(
            functools.partial(
                block_kernel, experts, pairs, halves, hot, cold, hidden_tile, weight_parts, grad_parts
            ),
            out_shape=[
                shape((rows, width), BF16),
                shape((rows, width), F32),
                shape((red_rows, width), F32),
                shape((width, hid), BF16),
                shape((hid, width), BF16),
                shape((width, hid), BF16),
                shape((hid, width), BF16),
            ],
            in_specs=[hbm, hbm, vmem, vmem, hbm, hbm, hbm, hbm, hbm],
            out_specs=[hbm, hbm, vmem, hbm, hbm, hbm, hbm],
            scratch_shapes=[
                pltpu.VMEM((rows, width), BF16),
                pltpu.VMEM((rows, width), BF16),
                pltpu.VMEM((rows, TILE), F32),
                pltpu.VMEM((2, width, hid), BF16),
                pltpu.VMEM((2, hid, width), BF16),
                pltpu.VMEM((rows, width), BF16),
                pltpu.VMEM((rows, width), F32),
                pltpu.VMEM((both, width), BF16),
                pltpu.VMEM((both, width), BF16),
                pltpu.VMEM((both, 2 * hid), BF16),
                pltpu.VMEM((both, 2 * hid), BF16),
                pltpu.VMEM((width, hid), BF16),
                pltpu.VMEM((hid, width), BF16),
                pltpu.VMEM((width, hid), BF16),
                pltpu.VMEM((hid, width), BF16),
                pltpu.VMEM((2, 2, cap, width), BF16),
                pltpu.VMEM((slot_rows, width), BF16),
                pltpu.VMEM((slot_rows, width), BF16),
                pltpu.VMEM((hid // grad_parts, width), F32),
                pltpu.VMEM((cap, width), F32),
                pltpu.VMEM((width // grad_parts, hid), F32),
                pltpu.VMEM((rows, experts), F32),
                pltpu.VMEM((slot_rows, width), BF16),
                pltpu.VMEM((slot_rows, width), BF16),
                pltpu.VMEM((red_rows, width), F32),
                pltpu.VMEM((pairs * halves, red_rows, width), F32),
                pltpu.VMEM((experts, red_rows, width), F32),
                sem((weight_parts,)), sem((weight_parts,)), sem((weight_parts,)), sem((weight_parts,)),
                sem((2, experts)), sem((2, experts)), sem((2, experts)), sem((2, experts)),
                sem((2, experts)), sem((2, experts)), sem((2, experts)), sem((2, experts)),
                sem((2, grad_pieces)), sem((2, grad_pieces)), sem((2, grad_pieces)), sem((2, grad_pieces)),
                sem((peers,)), sem((peers,)), sem((7,)), sem((2, grad_pieces)), sem((2, rows // SMALL)),
                pltpu.SemaphoreType.REGULAR,
            ],
            compiler_params=params(collective_id=1 + (experts if hot is None else hot)),
        )

    operands = (tokens, aux, gain_row, router_rows, w_in[0], w_out[0], cotangent, bn, bg)
    if experts <= 4:
        branches = [block(e) for e in range(experts)] + [block(None)]
        out = lax.switch(level[0], branches, *operands)
    else:
        out = block(None)(*operands)
    act, ig, red, ga_in, ga_out, gb_in, gb_out = out
    if pairs > 2:
        first, second = lax.psum((ga_in.astype(F32), ga_out.astype(F32)), "dp")
        return act, ig, red[experts], red[:experts].T, first[None], second[None]

    steps = 8

    def blocked(array):
        return pl.BlockSpec((array.shape[0] // steps, array.shape[1]), lambda i: (i, 0))

    def whole(array):
        return pl.BlockSpec(array.shape, lambda i: (0, 0))

    outs = [
        shape((rows, width), BF16),
        shape((rows, width), F32),
        shape((1, width), F32),
        shape((experts, width), F32),
        shape((width, hid), F32),
        shape((hid, width), F32),
    ]
    act, ig, gain_grad, router_grad, first, second = pl.pallas_call(
        functools.partial(finish_kernel, experts),
        grid=(steps,),
        out_shape=outs,
        in_specs=[blocked(act), blocked(ig), whole(red)] + [blocked(a) for a in (ga_in, ga_out, gb_in, gb_out)],
        out_specs=[blocked(outs[0]), blocked(outs[1]), whole(outs[2]), whole(outs[3]), blocked(outs[4]), blocked(outs[5])],
    )(act, ig, red, ga_in, ga_out, gb_in, gb_out)
    return act, ig, gain_grad[0], router_grad.T, first[None], second[None]


def solution(mesh):
    placed = (
        P(AXES, None),
        P(AXES, None),
        P(),
        P(),
        P("expert", None, "hidden"),
        P("expert", "hidden", None),
        P(AXES, None),
    )
    return jax.shard_map(
        on_device,
        mesh=mesh,
        in_specs=placed,
        out_specs=(
            P(AXES, None),
            P(AXES, None),
            P(),
            P(),
            P("expert", None, "hidden"),
            P("expert", "hidden", None),
        ),
        check_vma=False,
    )
```

```python
import functools

import jax
import jax.numpy as jnp
from jax import lax
from jax.experimental import pallas as pl
from jax.experimental.pallas import tpu as pltpu
from jax.sharding import PartitionSpec as P

HIGHEST = lax.Precision.HIGHEST
MESH = pl.DeviceIdType.MESH
EPSILON = 1e-05
F32 = jnp.float32
BF16 = jnp.bfloat16
AXES = ("dp", "expert", "hidden")
C0 = 0.7978845608
C1 = 0.044715
TILE = 128
PIECE = 128
SMALL = 64


def flip(index, mask, limit):
    out, bit = 0, 1
    while bit < limit:
        a, b = lax.rem(lax.div(index, bit), 2), lax.rem(lax.div(mask, bit), 2)
        out = out + bit * (a + b - 2 * a * b)
        bit *= 2
    return out


def one_row(ref):
    return jnp.concatenate([ref[i:i + 1, :].astype(F32) for i in range(ref.shape[0])], axis=1)


def contract(a, b, left, right, **kwargs):
    return lax.dot_general(a, b, (((left,), (right,)), ((), ())), preferred_element_type=F32, **kwargs)


def dot_nn(a, b):
    return contract(a, b, 1, 0)


def dot_nt(a, b):
    return contract(a, b, 1, 1)


def dot_tn(a, b):
    return contract(a, b, 0, 0)


def remote(src, dst, send, recv, peer):
    return pltpu.make_async_remote_copy(
        src_ref=src, dst_ref=dst, send_sem=send, recv_sem=recv, device_id=peer, device_id_type=MESH
    )


def plane_peer(i, pairs, halves):
    dp, z, h = (lax.axis_index(a) for a in AXES)
    return lax.rem(dp + lax.div(i, halves), pairs), z, lax.rem(h + lax.rem(i, halves), halves)


def line_peer(i, experts):
    dp, z, h = (lax.axis_index(a) for a in AXES)
    return dp, lax.rem(z + i, experts), h


def signal_all(pairs, experts, halves):
    barrier = pltpu.get_barrier_semaphore()

    @pl.loop(1, pairs * halves)
    def _(i):
        pl.semaphore_signal(barrier, inc=1, device_id=plane_peer(i, pairs, halves), device_id_type=MESH)

    @pl.loop(1, experts)
    def _(i):
        pl.semaphore_signal(barrier, inc=1, device_id=line_peer(i, experts), device_id_type=MESH)


def wait_all(pairs, experts, halves):
    pl.semaphore_wait(pltpu.get_barrier_semaphore(), pairs * halves + experts - 2)


def prologue_kernel(
    experts, pairs, halves, cold,
    x_hbm, route_ref, gain_ref, router_ref, cot_hbm,
    bn_out, bg_out, aux_ref, level_ref,
    x_ref, cot_ref, place, router, ranks, marks, stage, counts, count_in, line_in, send, recv, load, local,
):
    tokens, width = x_ref.shape
    cap = bn_out.shape[0] // experts
    signal_all(pairs, experts, halves)
    loads = [
        pltpu.make_async_copy(src, dst, load.at[i])
        for i, (src, dst) in enumerate(((x_hbm, x_ref), (cot_hbm, cot_ref)))
    ]
    for copy in loads:
        copy.start()

    lane = lax.broadcasted_iota(jnp.int32, (tokens, TILE), 1)
    chosen = jnp.transpose(jnp.broadcast_to(route_ref[...].astype(F32), (TILE, tokens)))
    onehot = (chosen.astype(jnp.int32) == lane).astype(F32)
    counts[...] = jnp.broadcast_to(jnp.sum(onehot, axis=0, keepdims=True), (8, TILE))
    ranks[0] = chosen
    marks[...] = onehot.astype(BF16)

    @pl.loop(0, tokens // TILE)
    def _(i):
        rows = pl.ds(pl.multiple_of(i * TILE, TILE), TILE)
        before = (
            lax.broadcasted_iota(jnp.int32, (TILE, tokens), 1)
            < lax.broadcasted_iota(jnp.int32, (TILE, tokens), 0) + i * TILE
        ).astype(BF16)
        rank = jnp.sum(dot_nn(before, marks[...]) * marks[rows, :].astype(F32), axis=1, keepdims=True)
        ranks[1, rows, :] = ranks[0, rows, :] * cap + rank

    router[...] = jnp.zeros_like(router)
    router[pl.ds(0, experts), :] = router_ref[...]

    here = pairs * halves

    def plane_copy(i):
        return remote(counts, count_in.at[i], send.at[i], recv.at[i], plane_peer(i, pairs, halves))

    def line_copy(i):
        at = here - 1 + i
        return remote(count_in.at[0], line_in.at[i], send.at[at], recv.at[at], line_peer(i, experts))

    wait_all(pairs, experts, halves)

    @pl.loop(1, here)
    def _(i):
        plane_copy(i).start()

    for copy in loads:
        copy.wait()

    @pl.loop(0, tokens // TILE)
    def _(i):
        rows = pl.ds(pl.multiple_of(i * TILE, TILE), TILE)
        x = x_ref[rows, :].astype(F32)
        inverse = lax.rsqrt(jnp.mean(x * x, axis=1, keepdims=True) + EPSILON)
        low = (x * inverse * one_row(gain_ref)).astype(BF16)
        x_ref[rows, :] = low
        lanes = lax.broadcasted_iota(jnp.int32, (TILE, TILE), 1)
        expert, slot = ranks[0, rows, :], ranks[1, rows, :]
        logits = jnp.where(lanes < experts, dot_nt(low, router[...]), -jnp.inf)
        shifted = jnp.exp(logits - jnp.max(logits, axis=1, keepdims=True))
        soft = shifted / jnp.sum(shifted, axis=1, keepdims=True)
        gate = jnp.sum(jnp.where(expert.astype(jnp.int32) == lanes, soft, 0.0), axis=1, keepdims=True)
        cot_ref[rows, :] = (gate * cot_ref[rows, :].astype(F32)).astype(BF16)
        aux = jnp.where(lanes == experts, gate, soft)
        aux = jnp.where(lanes == experts + 1, inverse, aux)
        aux = jnp.where(lanes == experts + 2, slot, aux)
        aux_ref[rows, :] = jnp.where(lanes == experts + 3, expert, aux)
        slot_int = slot.astype(jnp.int32)

        @pl.loop(0, experts * cap // TILE)
        def _(j):
            at = pl.ds(pl.multiple_of(j * TILE, TILE), TILE)
            place[rows, at] = (slot_int == lanes + j * TILE).astype(BF16)

    most = counts[...]
    for i in range(1, here):
        plane_copy(i).wait_recv()
        most = jnp.maximum(most, count_in[i])
    count_in[0] = most

    @pl.loop(1, experts)
    def _(i):
        line_copy(i).start()

    def out_copy(t, e):
        span = pl.ds(pl.multiple_of(e * cap, cap), cap)
        return pltpu.make_async_copy(stage.at[t, span], (bn_out, bg_out)[t].at[span], local.at[t, e])

    @pl.loop(0, experts)
    def _(e):
        span = pl.ds(pl.multiple_of(e * cap, cap), cap)
        for t, values in enumerate((x_ref, cot_ref)):
            stage[t, span, :] = dot_tn(place[:, span], values[...]).astype(BF16)
            out_copy(t, e).start()

    most = count_in[0]
    for i in range(1, experts):
        line_copy(i).wait_recv()
        most = jnp.maximum(most, line_in[i])
    lanes = lax.broadcasted_iota(jnp.int32, (8, TILE), 1)
    rows = lax.broadcasted_iota(jnp.int32, (8, TILE), 0)
    over = jnp.where((most > cold) & (rows == 0), 1.0, 0.0)
    crowded = jnp.sum(over)
    which = jnp.sum(over * lanes.astype(F32))
    level_ref[0] = jnp.where(crowded <= 1.0, which, float(experts)).astype(jnp.int32)

    @pl.loop(1, here)
    def _(i):
        plane_copy(i).wait_send()

    @pl.loop(1, experts)
    def _(i):
        line_copy(i).wait_send()

    @pl.loop(0, experts)
    def _(e):
        for t in (0, 1):
            out_copy(t, e).wait()


def block_kernel(
    experts, pairs, halves, hot, cold, hidden_tile, weight_parts, grad_parts,
    x_hbm, aux_hbm, gain_ref, router_ref, win_hbm, wout_hbm, cot_hbm, bn, bg,
    act_hbm, ig_hbm, red_ref, ga_in, ga_out, gb_in, gb_out,
    x_ref, cot_ref, aux_ref, w_in, w_out, act_ref, ig_ref,
    xs, gs, hs, ps, g_in, g_out, y_in, y_out,
    rs_send, rs_n, rs_g, acc_n, acc_g, acc_in, logits, ret_n, ret_g, total, red_plane, red_line,
    w_send, w_recv, wf_send, wf_recv, z_send, z_recv, f_send, f_recv, r_send, r_recv,
    b_send, b_recv, y_send, y_recv, d_send, d_recv, red_send, red_recv, load, local, out_sem, all_in,
):
    tokens, width = x_ref.shape
    hid = w_in.shape[2]
    cap = bn.shape[0] // experts
    dp, z, h = (lax.axis_index(a) for a in AXES)
    c = lax.rem(h, 2)
    parity = lax.rem(dp, 2)
    core_peer = (dp, z, flip(h, 1, halves))
    y_peer = (dp, z, flip(h, 2, halves))
    x_peer = (flip(dp, 1, pairs), z, h)
    here = pairs * halves
    signal_all(pairs, experts, halves)
    wait_all(pairs, experts, halves)

    def sized(e, act):
        if hot is None:
            act(cap)
        else:
            @pl.when(e == hot)
            def _():
                act(cap)

            @pl.when(e != hot)
            def _():
                act(cold)

    def slots(e, rows=cap):
        return pl.ds(pl.multiple_of(e * cap, cap), rows)

    def arrive(source, core, rows=cap):
        return pl.ds(pl.multiple_of((source * 2 + core) * cap, cap), rows)

    def turn_k(turn):
        return flip(turn, lax.div(turn, 2), experts)

    def z_copy(t, k, rows):
        src, dst = ((bn, xs), (bg, gs))[t]
        e = flip(z, k, experts)
        return remote(
            src.at[slots(e, rows)], dst.at[arrive(z, c, rows)], z_send.at[t, k], z_recv.at[t, k], (dp, e, h)
        )

    def z_start(t, k):
        sized(flip(z, k, experts), lambda rows: z_copy(t, k, rows).start())

    order = sorted(range(1, experts), key=lambda k: (k != experts - 1, k))
    for k in order:
        for t in (0, 1):
            z_start(t, k)

    mats = ((win_hbm, w_in), (wout_hbm, w_out))

    def weight_copy(which, part):
        src, dst = mats[which]
        rows = src.shape[0] // weight_parts
        span = pl.ds(pl.multiple_of(part * rows, rows), rows)
        return remote(src.at[span], dst.at[1, span], w_send.at[part], w_recv.at[part], y_peer)

    def weight_pass(which, part):
        dst = mats[which][1]
        rows = dst.shape[1] // weight_parts
        span = pl.ds(pl.multiple_of(part * rows, rows), rows)
        return remote(dst.at[1, span], dst.at[1, span], wf_send.at[part], wf_recv.at[part], x_peer)

    for which in (0, 1):
        @pl.when(parity == which)
        def _():
            @pl.loop(0, weight_parts)
            def _(part):
                weight_copy(which, part).start()

    def pair_copy(t, k, rows):
        buf = (xs, gs)[t]
        span = arrive(flip(z, k, experts), c, rows)
        return remote(buf.at[span], buf.at[span], f_send.at[t, k], f_recv.at[t, k], core_peer)

    def own_pair(t, rows):
        src, dst = ((bn, xs), (bg, gs))[t]
        return remote(
            src.at[slots(z, rows)], dst.at[arrive(z, c, rows)], f_send.at[t, 0], f_recv.at[t, 0], core_peer
        )

    def own_local(t, rows):
        src, dst = ((bn, xs), (bg, gs))[t]
        return pltpu.make_async_copy(src.at[slots(z, rows)], dst.at[arrive(z, c, rows)], load.at[t])

    for t in (0, 1):
        sized(z, lambda rows: own_pair(t, rows).start())
        sized(z, lambda rows: own_local(t, rows).start())
    loads = [
        pltpu.make_async_copy(src, dst, load.at[2 + i])
        for i, (src, dst) in enumerate(
            (
                (win_hbm, w_in.at[0]), (wout_hbm, w_out.at[0]),
                (x_hbm, x_ref), (cot_hbm, cot_ref), (aux_hbm, aux_ref),
            )
        )
    ]
    for copy in loads:
        copy.start()

    if hot is not None:
        @pl.when(z != hot)
        def _():
            @pl.loop(0, 2 * experts)
            def _(i):
                rest = pl.ds(pl.multiple_of(i * cap, cap) + cold, cap - cold)
                xs[rest, :] = jnp.zeros((cap - cold, width), BF16)
                gs[rest, :] = jnp.zeros((cap - cold, width), BF16)

        @pl.loop(0, experts)
        def _(e):
            @pl.when(e != hot)
            def _():
                rest = pl.ds(pl.multiple_of(e * cap, cap) + cold, cap - cold)
                ret_n[rest, :] = jnp.zeros((cap - cold, width), BF16)
                ret_g[rest, :] = jnp.zeros((cap - cold, width), BF16)

    for copy in loads:
        copy.wait()
    for t in (0, 1):
        sized(z, lambda rows: own_local(t, rows).wait())

    def other_weights():
        for which in (0, 1):
            @pl.when(parity == which)
            def _():
                @pl.loop(0, weight_parts)
                def _(part):
                    weight_copy(which, part).wait_recv()
                    weight_pass(which, part).start()

                @pl.loop(0, weight_parts)
                def _(part):
                    weight_pass(1 - which, part).wait_recv()
                    weight_copy(which, part).wait_send()
                    weight_pass(which, part).wait_send()

    per_half = hid // hidden_tile

    def rows_in(turn):
        k = turn_k(turn)

        @pl.when(turn > 0)
        def _():
            for t in (0, 1):
                sized(z, lambda rows: z_copy(t, k, rows).wait_recv())
                sized(z, lambda rows: pair_copy(t, k, rows).start())

        @pl.when(turn == experts - 1)
        def _():
            @pl.loop(1, experts)
            def _(i):
                pl.semaphore_signal(all_in, inc=1, device_id=line_peer(i, experts), device_id_type=MESH)

        for t in (0, 1):
            sized(z, lambda rows: pair_copy(t, k, rows).wait_recv())

    def token_block(turn, first, last):
        source = flip(z, turn_k(turn), experts)
        chunk = pl.ds(pl.multiple_of(source * 2 * cap, 2 * cap), 2 * cap)

        @pl.loop(first, last)
        def _(j):
            half = lax.div(j, per_half)
            cols = pl.ds(pl.multiple_of(lax.rem(j, per_half) * hidden_tile, hidden_tile), hidden_tile)
            pre = dot_nn(xs[chunk, :], w_in[half, :, cols])
            back = dot_nt(gs[chunk, :], w_out[half, cols, :])
            square = pre * pre
            curve = jnp.tanh(pre * (C0 + (C0 * C1) * square))
            low_half = 0.5 + 0.5 * curve
            slope = low_half + pre * (1.0 - curve * curve) * (0.5 * C0 + (1.5 * C0 * C1) * square)
            at = pl.ds(pl.multiple_of(j * hidden_tile, hidden_tile), hidden_tile)
            hs[chunk, at] = (pre * low_half).astype(BF16)
            ps[chunk, at] = (back * slope).astype(BF16)

    def rs_copy(t, k, slot):
        return remote(
            rs_send.at[slot, t], (rs_n, rs_g)[t].at[slots(k)], r_send.at[t, k], r_recv.at[t, k], core_peer
        )

    def back_copy(t, k, rows):
        src, dst = ((rs_n, ret_n), (rs_g, ret_g))[t]
        return remote(
            src.at[slots(k, rows)], dst.at[slots(z, rows)], b_send.at[t, k], b_recv.at[t, k],
            (dp, flip(z, k, experts), h),
        )

    def back_start(turn):
        k = turn_k(turn)
        for t in (0, 1):
            sized(z, lambda rows: back_copy(t, k, rows).start())

    def held(turn):
        if hot is None:
            back_start(turn)
        else:
            @pl.when(z != hot)
            def _():
                back_start(turn)

    def token_sums(turn):
        k = turn_k(turn)
        source = flip(z, k, experts)
        place_in = lax.rem(turn + experts - 1, experts)
        slot = lax.rem(place_in, 2)

        @pl.when(place_in >= 2)
        def _():
            for t in (0, 1):
                rs_copy(t, turn_k(place_in - 1), slot).wait_send()

        @pl.loop(0, 2)
        def _(mine):
            rows = arrive(source, lax.rem(1 + c + mine, 2))
            for t, (values, weights, dot, acc) in enumerate(
                ((hs, w_out, dot_nn, acc_n), (ps, w_in, dot_nt, acc_g))
            ):
                acc = acc.at[pl.ds(0, cap)]
                acc[...] = jnp.zeros_like(acc)

                @pl.loop(0, 2)
                def _(half):
                    cols = pl.ds(pl.multiple_of(half * hid, hid), hid)
                    acc[...] += dot(values[rows, cols], weights[half])

                @pl.when(mine == 0)
                def _():
                    rs_send[slot, t] = acc[...].astype(BF16)
                    rs_copy(t, k, slot).start()

        for t, (acc, got, home) in enumerate(((acc_n, rs_n, ret_n), (acc_g, rs_g, ret_g))):
            rs_copy(t, k, slot).wait_recv()
            both = (acc[pl.ds(0, cap), :] + got[slots(k), :].astype(F32)).astype(BF16)

            @pl.when(turn == 0)
            def _():
                home[slots(z), :] = both

            @pl.when(turn > 0)
            def _():
                got[slots(k), :] = both

    heights = (width // grad_parts, hid // grad_parts)
    subs = tuple(height // PIECE for height in heights)

    def grad_span(t, i, sub=None):
        if sub is None:
            return pl.ds(pl.multiple_of(i * heights[t], heights[t]), heights[t])
        return pl.ds(pl.multiple_of(i * heights[t] + sub * PIECE, PIECE), PIECE)

    def y_copy(t, i, sub):
        src, dst = ((g_in, y_in), (g_out, y_out))[t]
        span, at = grad_span(t, i, sub), i * subs[t] + sub
        return remote(src.at[span], dst.at[span], y_send.at[t, at], y_recv.at[t, at], y_peer)

    def d_copy(t, i, sub):
        src, dst = ((y_in, gb_in), (y_out, gb_out))[t]
        span, at = grad_span(t, i, sub), i * subs[t] + sub
        return remote(src.at[span], dst.at[span], d_send.at[t, at], d_recv.at[t, at], x_peer)

    def d_local(t, i, sub):
        src, dst = ((y_in, ga_in), (y_out, ga_out))[t]
        span, at = grad_span(t, i, sub), i * subs[t] + sub
        return pltpu.make_async_copy(src.at[span], dst.at[span], local.at[t, at])

    accs = (acc_in, acc_n)

    def weight_grad(t, i, half):
        accs[t][...] = jnp.zeros_like(accs[t])
        depth = 2 * cap
        at = pl.ds(pl.multiple_of(half * hid, hid), hid)
        if t:
            at = pl.ds(pl.multiple_of(half * hid + i * heights[1], heights[1]), heights[1])

        @pl.loop(0, experts)
        def _(n):
            rows = pl.ds(pl.multiple_of(n * depth, depth), depth)
            if t == 0:
                accs[t][...] += dot_tn(xs[rows, grad_span(0, i)], ps[rows, at])
            else:
                accs[t][...] += dot_tn(hs[rows, at], gs[rows, :])

    place = hs.at[pl.ds(0, tokens), pl.ds(0, experts * cap)]
    got_n = ps.at[pl.ds(0, tokens), pl.ds(0, width)]
    got_g = ps.at[pl.ds(tokens, tokens), pl.ds(0, width)]
    normed = hs.at[pl.ds(tokens, tokens), pl.ds(0, width)]

    def unbucket():
        @pl.loop(0, tokens // TILE)
        def _(i):
            rows = pl.ds(pl.multiple_of(i * TILE, TILE), TILE)
            slot = aux_ref[rows, experts + 2:experts + 3].astype(jnp.int32)
            lanes = lax.broadcasted_iota(jnp.int32, (TILE, experts * cap), 1)
            place[rows, :] = (slot == lanes).astype(BF16)

        @pl.loop(0, 3)
        def _(n):
            cols = pl.ds(pl.multiple_of(n * (width // 3), width // 3), width // 3)

            @pl.loop(0, tokens // TILE)
            def _(m):
                rows = pl.ds(pl.multiple_of(m * TILE, TILE), TILE)
                got_n[rows, cols] = dot_nn(place[rows, :], ret_n[:, cols]).astype(BF16)
                got_g[rows, cols] = dot_nn(place[rows, :], ret_g[:, cols]).astype(BF16)

    def out_copy(t, i):
        rows = pl.ds(pl.multiple_of(i * SMALL, SMALL), SMALL)
        src, dst = ((act_ref, act_hbm), (ig_ref, ig_hbm))[t]
        return pltpu.make_async_copy(src.at[rows], dst.at[rows], out_sem.at[t, i])

    def tokens_tile(i):
        rows = pl.ds(pl.multiple_of(i * SMALL, SMALL), SMALL)
        aux = aux_ref[rows, :]
        soft, g, inverse = aux[:, :experts], aux[:, experts:experts + 1], aux[:, experts + 1:experts + 2]
        chosen = aux[:, experts + 3:experts + 4].astype(jnp.int32)
        expert_out = got_n[rows, :].astype(F32)
        expert_g = got_g[rows, :].astype(F32)
        x = x_ref[rows, :].astype(F32)
        up = cot_ref[rows, :].astype(F32)
        gain = one_row(gain_ref)
        hits = (chosen == lax.broadcasted_iota(jnp.int32, (SMALL, experts), 1)).astype(F32)
        act_ref[rows, :] = (x + g * expert_out).astype(BF16)
        out_copy(0, i).start()
        gate_g = jnp.sum(up * expert_out, axis=1, keepdims=True)
        logit_g = gate_g * g * (hits - soft)
        logits[rows, :] = logit_g
        normed[rows, :] = (x * inverse * gain).astype(BF16)
        normed_g = expert_g
        for e in range(experts):
            normed_g = normed_g + logit_g[:, e:e + 1] * router_ref[e:e + 1, :].astype(F32)
        total[pl.ds(experts, 1), :] += jnp.sum(normed_g * x * inverse, axis=0, keepdims=True)
        u = gain * normed_g
        dot = jnp.sum(u * x, axis=1, keepdims=True)
        ig_ref[rows, :] = up + inverse * u - x * (inverse * inverse * inverse * dot / width)
        out_copy(1, i).start()

    def router_sum():
        rest = logits[...]
        added = jnp.zeros((experts, width), F32)
        for _ in range(3):
            term = rest.astype(BF16)
            added = added + dot_tn(term, normed[...])
            rest = rest - term.astype(F32)
        total[pl.ds(0, experts), :] = added

    def returned():
        @pl.loop(1, experts)
        def _(turn):
            k = turn_k(turn)
            for t in (0, 1):
                sized(flip(z, k, experts), lambda rows: back_copy(t, k, rows).wait_recv())

    def red_plane_copy(i):
        peer = plane_peer(i, pairs, halves)
        return remote(total, red_plane.at[dp * halves + h], red_send.at[i], red_recv.at[i], peer)

    def red_line_copy(i):
        at = here - 1 + i
        return remote(total, red_line.at[z], red_send.at[at], red_recv.at[at], line_peer(i, experts))

    def token_results():
        returned()
        unbucket()
        total[...] = jnp.zeros_like(total)

        @pl.loop(0, tokens // SMALL)
        def _(i):
            tokens_tile(i)

        router_sum()
        red_plane[dp * halves + h] = total[...]

        @pl.loop(1, here)
        def _(i):
            red_plane_copy(i).start()

    def plane_sum():
        @pl.loop(1, here)
        def _(i):
            red_plane_copy(i).wait()

        added = red_plane[0]
        for i in range(1, here):
            added = added + red_plane[i]
        total[...] = added
        red_line[z] = added

        @pl.loop(1, experts)
        def _(i):
            red_line_copy(i).start()

    plans = (((1, 0), (0, 0), (1, 1), (1, 2), (0, 1), (0, 2)), ((1, 0), (1, 1), (0, 0), (1, 2), (0, 1), (0, 2)))
    late_steps = len(plans[0])

    def planned(t, step, what):
        return sum(jnp.where(step == n, plan[what], 0) for n, plan in enumerate(plans[t]))

    def grad_form(t, step):
        weight_grad(t, planned(t, step, 1), planned(t, step, 0))

    def grad_pass(t, step):
        half, i = planned(t, step, 0), planned(t, step, 1)
        out, got = ((g_in, y_in), (g_out, y_out))[t]

        @pl.when(half == 1)
        def _():
            out[grad_span(t, i), :] = accs[t][...].astype(BF16)

            @pl.loop(0, subs[t])
            def _(sub):
                y_copy(t, i, sub).start()

        @pl.when(half == 0)
        def _():
            @pl.loop(0, subs[t])
            def _(sub):
                if t:
                    @pl.when((step == late_steps - 1) & (sub == subs[1] - 1))
                    def _():
                        token_results()

                span = grad_span(t, i, sub)
                y_copy(t, i, sub).wait_recv()
                mine = accs[t][pl.ds(pl.multiple_of(sub * PIECE, PIECE), PIECE), :]
                got[span, :] = (mine + got[span, :].astype(F32)).astype(BF16)
                if pairs == 2:
                    d_copy(t, i, sub).start()
                d_local(t, i, sub).start()

    @pl.loop(0, experts + 1 + late_steps)
    def _(step):
        late = step - experts - 1

        @pl.when(late >= 0)
        def _():
            grad_form(0, late)

        @pl.when(((step > 2) & (step <= experts)) | (late == 1) | (late == 3))
        def _():
            token_sums(jnp.where(step <= experts, step - 2, jnp.where(late == 1, experts - 1, 0)))

        @pl.when(late == 1)
        def _():
            back_start(experts - 1)

        if hot is not None:
            @pl.when((step > 2) & (step <= experts) & (z == hot))
            def _():
                back_start(step - 2)

        @pl.when(late >= 0)
        def _():
            grad_pass(0, late)

            @pl.when(late == 0)
            def _():
                pl.semaphore_wait(all_in, experts - 1)

                @pl.loop(1, experts - 1)
                def _(earlier):
                    held(earlier)

            grad_form(1, late)
            grad_pass(1, late)

        @pl.when(step == 1)
        def _():
            other_weights()

        turn = jnp.where(step < 2, 0, jnp.where(step <= experts, step - 1, experts - 1))

        @pl.when((step != 1) & (step <= experts))
        def _():
            rows_in(turn)

        @pl.when(step <= experts + 1)
        def _():
            token_block(
                turn,
                jnp.where((step == 1) | (step == experts), per_half, 0),
                jnp.where((step == 0) | (step == experts + 1), per_half, 2 * per_half),
            )

    plane_sum()

    @pl.loop(1, experts)
    def _(i):
        red_line_copy(i).wait()

    added = red_line[0]
    for i in range(1, experts):
        added = added + red_line[i]
    red_ref[...] = added

    @pl.loop(1, experts)
    def _(turn):
        k = turn_k(turn)
        for t in (0, 1):
            sized(flip(z, k, experts), lambda rows: z_copy(t, k, rows).wait_send())
            sized(z, lambda rows: pair_copy(t, k, rows).wait_send())
            sized(z, lambda rows: back_copy(t, k, rows).wait_send())
    for t in (0, 1):
        sized(z, lambda rows: own_pair(t, rows).wait_send())
        for place_in in range(max(0, experts - 2), experts):
            rs_copy(t, turn_k((place_in + 1) % experts), place_in % 2).wait_send()

    @pl.loop(0, tokens // SMALL)
    def _(i):
        for t in (0, 1):
            out_copy(t, i).wait()

    @pl.loop(0, grad_parts)
    def _(i):
        for t in (0, 1):
            @pl.loop(0, subs[t])
            def _(sub):
                y_copy(t, i, sub).wait_send()
                d_local(t, i, sub).wait()
                if pairs == 2:
                    d_copy(t, i, sub).wait()


def finish_kernel(experts, act, ig, red, ai, ao, bi, bo, act_out, ig_out, gain_out, router_out, first_out, second_out):
    act_out[...] = act[...]
    ig_out[...] = ig[...]
    first_out[...] = ai[...].astype(F32) + bi[...].astype(F32)
    second_out[...] = ao[...].astype(F32) + bo[...].astype(F32)

    @pl.when(pl.program_id(0) == 0)
    def _():
        for i in range(gain_out.shape[0]):
            gain_out[i:i + 1, :] = red[experts:experts + 1, i * TILE:(i + 1) * TILE]
        router_out[...] = red[pl.ds(0, experts), :]


def on_device(tokens, route, norm_gain, router_weight, w_in, w_out, cotangent):
    rows, width = tokens.shape
    experts = lax.axis_size("expert")
    pairs = lax.axis_size("dp")
    halves = lax.axis_size("hidden")
    cap = 2 * rows // experts
    hid = w_in.shape[2]
    cold = 16 * (-(-11 * cap // 256))
    hidden_tile = 256
    weight_parts, grad_parts = 12, 3
    grad_pieces = max(width, hid) // PIECE
    slot_rows = experts * cap
    both = 2 * slot_rows
    red_rows = 8 * ((experts + 1 + 7) // 8)
    peers = pairs * halves + experts
    vmem = pl.BlockSpec(memory_space=pltpu.VMEM)
    hbm = pl.BlockSpec(memory_space=pl.ANY)
    sem = pltpu.SemaphoreType.DMA
    shape = jax.ShapeDtypeStruct
    params = functools.partial(pltpu.CompilerParams, has_side_effects=True, vmem_limit_bytes=62 * 1024 * 1024)
    gain_row = norm_gain.reshape(width // TILE, TILE)
    router_rows = router_weight.T

    bn, bg, aux, level = pl.pallas_call(
        functools.partial(prologue_kernel, experts, pairs, halves, cold),
        out_shape=[
            shape((slot_rows, width), BF16),
            shape((slot_rows, width), BF16),
            shape((rows, TILE), F32),
            shape((1,), jnp.int32),
        ],
        in_specs=[hbm, vmem, vmem, vmem, hbm],
        out_specs=[hbm, hbm, vmem, pl.BlockSpec(memory_space=pltpu.SMEM)],
        scratch_shapes=[
            pltpu.VMEM((rows, width), BF16),
            pltpu.VMEM((rows, width), BF16),
            pltpu.VMEM((rows, slot_rows), BF16),
            pltpu.VMEM((TILE, width), BF16),
            pltpu.VMEM((2, rows, TILE), F32),
            pltpu.VMEM((rows, TILE), BF16),
            pltpu.VMEM((2, slot_rows, width), BF16),
            pltpu.VMEM((8, TILE), F32),
            pltpu.VMEM((pairs * halves, 8, TILE), F32),
            pltpu.VMEM((experts, 8, TILE), F32),
            sem((peers,)), sem((peers,)), sem((2,)), sem((2, experts)),
        ],
        compiler_params=params(collective_id=0),
    )(tokens, route.T, gain_row, router_rows, cotangent)

    def block(hot):
        return pl.pallas_call(
            functools.partial(
                block_kernel, experts, pairs, halves, hot, cold, hidden_tile, weight_parts, grad_parts
            ),
            out_shape=[
                shape((rows, width), BF16),
                shape((rows, width), F32),
                shape((red_rows, width), F32),
                shape((width, hid), BF16),
                shape((hid, width), BF16),
                shape((width, hid), BF16),
                shape((hid, width), BF16),
            ],
            in_specs=[hbm, hbm, vmem, vmem, hbm, hbm, hbm, hbm, hbm],
            out_specs=[hbm, hbm, vmem, hbm, hbm, hbm, hbm],
            scratch_shapes=[
                pltpu.VMEM((rows, width), BF16),
                pltpu.VMEM((rows, width), BF16),
                pltpu.VMEM((rows, TILE), F32),
                pltpu.VMEM((2, width, hid), BF16),
                pltpu.VMEM((2, hid, width), BF16),
                pltpu.VMEM((rows, width), BF16),
                pltpu.VMEM((rows, width), F32),
                pltpu.VMEM((both, width), BF16),
                pltpu.VMEM((both, width), BF16),
                pltpu.VMEM((both, 2 * hid), BF16),
                pltpu.VMEM((both, 2 * hid), BF16),
                pltpu.VMEM((width, hid), BF16),
                pltpu.VMEM((hid, width), BF16),
                pltpu.VMEM((width, hid), BF16),
                pltpu.VMEM((hid, width), BF16),
                pltpu.VMEM((2, 2, cap, width), BF16),
                pltpu.VMEM((slot_rows, width), BF16),
                pltpu.VMEM((slot_rows, width), BF16),
                pltpu.VMEM((hid // grad_parts, width), F32),
                pltpu.VMEM((cap, width), F32),
                pltpu.VMEM((width // grad_parts, hid), F32),
                pltpu.VMEM((rows, experts), F32),
                pltpu.VMEM((slot_rows, width), BF16),
                pltpu.VMEM((slot_rows, width), BF16),
                pltpu.VMEM((red_rows, width), F32),
                pltpu.VMEM((pairs * halves, red_rows, width), F32),
                pltpu.VMEM((experts, red_rows, width), F32),
                sem((weight_parts,)), sem((weight_parts,)), sem((weight_parts,)), sem((weight_parts,)),
                sem((2, experts)), sem((2, experts)), sem((2, experts)), sem((2, experts)),
                sem((2, experts)), sem((2, experts)), sem((2, experts)), sem((2, experts)),
                sem((2, grad_pieces)), sem((2, grad_pieces)), sem((2, grad_pieces)), sem((2, grad_pieces)),
                sem((peers,)), sem((peers,)), sem((7,)), sem((2, grad_pieces)), sem((2, rows // SMALL)),
                pltpu.SemaphoreType.REGULAR,
            ],
            compiler_params=params(collective_id=1 + (experts if hot is None else hot)),
        )

    operands = (tokens, aux, gain_row, router_rows, w_in[0], w_out[0], cotangent, bn, bg)
    if experts <= 4:
        branches = [block(e) for e in range(experts)] + [block(None)]
        out = lax.switch(level[0], branches, *operands)
    else:
        out = block(None)(*operands)
    act, ig, red, ga_in, ga_out, gb_in, gb_out = out
    if pairs > 2:
        first, second = lax.psum((ga_in.astype(F32), ga_out.astype(F32)), "dp")
        return act, ig, red[experts], red[:experts].T, first[None], second[None]

    steps = 2

    def blocked(array):
        return pl.BlockSpec((array.shape[0] // steps, array.shape[1]), lambda i: (i, 0))

    def whole(array):
        return pl.BlockSpec(array.shape, lambda i: (0, 0))

    outs = [
        shape((rows, width), BF16),
        shape((rows, width), F32),
        shape((width // TILE, TILE), F32),
        shape((experts, width), F32),
        shape((width, hid), F32),
        shape((hid, width), F32),
    ]
    act, ig, gain_grad, router_grad, first, second = pl.pallas_call(
        functools.partial(finish_kernel, experts),
        grid=(steps,),
        out_shape=outs,
        in_specs=[blocked(act), blocked(ig), whole(red)] + [blocked(a) for a in (ga_in, ga_out, gb_in, gb_out)],
        out_specs=[blocked(outs[0]), blocked(outs[1]), whole(outs[2]), whole(outs[3]), blocked(outs[4]), blocked(outs[5])],
    )(act, ig, red, ga_in, ga_out, gb_in, gb_out)
    return act, ig, gain_grad.reshape(width), router_grad.T, first[None], second[None]


def solution(mesh):
    placed = (
        P(AXES, None),
        P(AXES, None),
        P(),
        P(),
        P("expert", None, "hidden"),
        P("expert", "hidden", None),
        P(AXES, None),
    )
    return jax.shard_map(
        on_device,
        mesh=mesh,
        in_specs=placed,
        out_specs=(
            P(AXES, None),
            P(AXES, None),
            P(),
            P(),
            P("expert", None, "hidden"),
            P("expert", "hidden", None),
        ),
        check_vma=False,
    )
```

```python
import functools

import jax
import jax.numpy as jnp
from jax import lax
from jax.experimental import pallas as pl
from jax.experimental.pallas import tpu as pltpu
from jax.sharding import PartitionSpec as P

HIGHEST = lax.Precision.HIGHEST
MESH = pl.DeviceIdType.MESH
EPSILON = 1e-05
F32 = jnp.float32
BF16 = jnp.bfloat16
AXES = ("dp", "expert", "hidden")
C0 = 0.7978845608
C1 = 0.044715
TILE = 128
PIECE = 128
SMALL = 64


def flip(index, mask, limit):
    out, bit = 0, 1
    while bit < limit:
        a, b = lax.rem(lax.div(index, bit), 2), lax.rem(lax.div(mask, bit), 2)
        out = out + bit * (a + b - 2 * a * b)
        bit *= 2
    return out


def one_row(ref):
    return jnp.concatenate([ref[i:i + 1, :].astype(F32) for i in range(ref.shape[0])], axis=1)


def contract(a, b, left, right, **kwargs):
    return lax.dot_general(a, b, (((left,), (right,)), ((), ())), preferred_element_type=F32, **kwargs)


def dot_nn(a, b):
    return contract(a, b, 1, 0)


def dot_nt(a, b):
    return contract(a, b, 1, 1)


def dot_tn(a, b):
    return contract(a, b, 0, 0)


def remote(src, dst, send, recv, peer):
    return pltpu.make_async_remote_copy(
        src_ref=src, dst_ref=dst, send_sem=send, recv_sem=recv, device_id=peer, device_id_type=MESH
    )


def plane_peer(i, pairs, halves):
    dp, z, h = (lax.axis_index(a) for a in AXES)
    return lax.rem(dp + lax.div(i, halves), pairs), z, lax.rem(h + lax.rem(i, halves), halves)


def line_peer(i, experts):
    dp, z, h = (lax.axis_index(a) for a in AXES)
    return dp, lax.rem(z + i, experts), h


def signal_all(pairs, experts, halves):
    barrier = pltpu.get_barrier_semaphore()

    @pl.loop(1, pairs * halves)
    def _(i):
        pl.semaphore_signal(barrier, inc=1, device_id=plane_peer(i, pairs, halves), device_id_type=MESH)

    @pl.loop(1, experts)
    def _(i):
        pl.semaphore_signal(barrier, inc=1, device_id=line_peer(i, experts), device_id_type=MESH)


def wait_all(pairs, experts, halves):
    pl.semaphore_wait(pltpu.get_barrier_semaphore(), pairs * halves + experts - 2)


def prologue_kernel(
    experts, pairs, halves, cold,
    x_hbm, route_ref, gain_ref, router_ref, cot_hbm,
    bn_out, bg_out, aux_ref, level_ref,
    x_ref, cot_ref, place, router, ranks, marks, stage, counts, count_in, line_in, send, recv, load, local,
):
    tokens, width = x_ref.shape
    cap = bn_out.shape[0] // experts
    signal_all(pairs, experts, halves)
    loads = [
        pltpu.make_async_copy(src, dst, load.at[i])
        for i, (src, dst) in enumerate(((x_hbm, x_ref), (cot_hbm, cot_ref)))
    ]
    for copy in loads:
        copy.start()

    lane = lax.broadcasted_iota(jnp.int32, (tokens, TILE), 1)
    chosen = jnp.transpose(jnp.broadcast_to(route_ref[...].astype(F32), (TILE, tokens)))
    onehot = (chosen.astype(jnp.int32) == lane).astype(F32)
    counts[...] = jnp.broadcast_to(jnp.sum(onehot, axis=0, keepdims=True), (8, TILE))
    ranks[0] = chosen
    marks[...] = onehot.astype(BF16)

    @pl.loop(0, tokens // TILE)
    def _(i):
        rows = pl.ds(pl.multiple_of(i * TILE, TILE), TILE)
        before = (
            lax.broadcasted_iota(jnp.int32, (TILE, tokens), 1)
            < lax.broadcasted_iota(jnp.int32, (TILE, tokens), 0) + i * TILE
        ).astype(BF16)
        rank = jnp.sum(dot_nn(before, marks[...]) * marks[rows, :].astype(F32), axis=1, keepdims=True)
        ranks[1, rows, :] = ranks[0, rows, :] * cap + rank

    router[...] = jnp.zeros_like(router)
    router[pl.ds(0, experts), :] = router_ref[...]

    here = pairs * halves

    def plane_copy(i):
        return remote(counts, count_in.at[i], send.at[i], recv.at[i], plane_peer(i, pairs, halves))

    def line_copy(i):
        at = here - 1 + i
        return remote(count_in.at[0], line_in.at[i], send.at[at], recv.at[at], line_peer(i, experts))

    wait_all(pairs, experts, halves)

    @pl.loop(1, here)
    def _(i):
        plane_copy(i).start()

    for copy in loads:
        copy.wait()

    @pl.loop(0, tokens // TILE)
    def _(i):
        rows = pl.ds(pl.multiple_of(i * TILE, TILE), TILE)
        x = x_ref[rows, :].astype(F32)
        inverse = lax.rsqrt(jnp.mean(x * x, axis=1, keepdims=True) + EPSILON)
        low = (x * inverse * one_row(gain_ref)).astype(BF16)
        x_ref[rows, :] = low
        lanes = lax.broadcasted_iota(jnp.int32, (TILE, TILE), 1)
        expert, slot = ranks[0, rows, :], ranks[1, rows, :]
        logits = jnp.where(lanes < experts, dot_nt(low, router[...]), -jnp.inf)
        shifted = jnp.exp(logits - jnp.max(logits, axis=1, keepdims=True))
        soft = shifted / jnp.sum(shifted, axis=1, keepdims=True)
        gate = jnp.sum(jnp.where(expert.astype(jnp.int32) == lanes, soft, 0.0), axis=1, keepdims=True)
        cot_ref[rows, :] = (gate * cot_ref[rows, :].astype(F32)).astype(BF16)
        aux = jnp.where(lanes == experts, gate, soft)
        aux = jnp.where(lanes == experts + 1, inverse, aux)
        aux = jnp.where(lanes == experts + 2, slot, aux)
        aux_ref[rows, :] = jnp.where(lanes == experts + 3, expert, aux)
        slot_int = slot.astype(jnp.int32)

        @pl.loop(0, experts * cap // TILE)
        def _(j):
            at = pl.ds(pl.multiple_of(j * TILE, TILE), TILE)
            place[rows, at] = (slot_int == lanes + j * TILE).astype(BF16)

    most = counts[...]
    for i in range(1, here):
        plane_copy(i).wait_recv()
        most = jnp.maximum(most, count_in[i])
    count_in[0] = most

    @pl.loop(1, experts)
    def _(i):
        line_copy(i).start()

    def out_copy(t, e):
        span = pl.ds(pl.multiple_of(e * cap, cap), cap)
        return pltpu.make_async_copy(stage.at[t, span], (bn_out, bg_out)[t].at[span], local.at[t, e])

    @pl.loop(0, experts)
    def _(e):
        span = pl.ds(pl.multiple_of(e * cap, cap), cap)
        for t, values in enumerate((x_ref, cot_ref)):
            stage[t, span, :] = dot_tn(place[:, span], values[...]).astype(BF16)
            out_copy(t, e).start()

    most = count_in[0]
    for i in range(1, experts):
        line_copy(i).wait_recv()
        most = jnp.maximum(most, line_in[i])
    lanes = lax.broadcasted_iota(jnp.int32, (8, TILE), 1)
    rows = lax.broadcasted_iota(jnp.int32, (8, TILE), 0)
    over = jnp.where((most > cold) & (rows == 0), 1.0, 0.0)
    crowded = jnp.sum(over)
    which = jnp.sum(over * lanes.astype(F32))
    level_ref[0] = jnp.where(crowded <= 1.0, which, float(experts)).astype(jnp.int32)

    @pl.loop(1, here)
    def _(i):
        plane_copy(i).wait_send()

    @pl.loop(1, experts)
    def _(i):
        line_copy(i).wait_send()

    @pl.loop(0, experts)
    def _(e):
        for t in (0, 1):
            out_copy(t, e).wait()


def block_kernel(
    experts, pairs, halves, hot, cold, hidden_tile, weight_parts, grad_parts,
    x_hbm, aux_hbm, gain_ref, router_ref, win_hbm, wout_hbm, cot_hbm, bn, bg,
    act_hbm, ig_hbm, red_ref, ga_in, ga_out, gb_in, gb_out,
    x_ref, cot_ref, aux_ref, w_in, w_out, act_ref, ig_ref,
    xs, gs, hs, ps, g_in, g_out, y_in, y_out,
    rs_send, rs_n, rs_g, acc_n, acc_g, acc_in, logits, ret_n, ret_g, total, red_plane, red_line,
    w_send, w_recv, wf_send, wf_recv, z_send, z_recv, f_send, f_recv, r_send, r_recv,
    b_send, b_recv, y_send, y_recv, d_send, d_recv, red_send, red_recv, load, local, out_sem,
):
    tokens, width = x_ref.shape
    hid = w_in.shape[2]
    cap = bn.shape[0] // experts
    dp, z, h = (lax.axis_index(a) for a in AXES)
    c = lax.rem(h, 2)
    parity = lax.rem(dp, 2)
    core_peer = (dp, z, flip(h, 1, halves))
    y_peer = (dp, z, flip(h, 2, halves))
    x_peer = (flip(dp, 1, pairs), z, h)
    here = pairs * halves
    signal_all(pairs, experts, halves)
    wait_all(pairs, experts, halves)

    def sized(e, act):
        if hot is None:
            act(cap)
        else:
            @pl.when(e == hot)
            def _():
                act(cap)

            @pl.when(e != hot)
            def _():
                act(cold)

    def slots(e, rows=cap):
        return pl.ds(pl.multiple_of(e * cap, cap), rows)

    def arrive(source, core, rows=cap):
        return pl.ds(pl.multiple_of((source * 2 + core) * cap, cap), rows)

    def turn_k(turn):
        return flip(turn, lax.div(turn, 2), experts)

    def z_copy(t, k, rows):
        src, dst = ((bn, xs), (bg, gs))[t]
        e = flip(z, k, experts)
        return remote(
            src.at[slots(e, rows)], dst.at[arrive(z, c, rows)], z_send.at[t, k], z_recv.at[t, k], (dp, e, h)
        )

    def z_start(t, k):
        sized(flip(z, k, experts), lambda rows: z_copy(t, k, rows).start())

    order = sorted(range(1, experts), key=lambda k: (k != experts - 1, k))
    for k in order:
        for t in (0, 1):
            z_start(t, k)

    mats = ((win_hbm, w_in), (wout_hbm, w_out))

    def weight_copy(which, part):
        src, dst = mats[which]
        rows = src.shape[0] // weight_parts
        span = pl.ds(pl.multiple_of(part * rows, rows), rows)
        return remote(src.at[span], dst.at[1, span], w_send.at[part], w_recv.at[part], y_peer)

    def weight_pass(which, part):
        dst = mats[which][1]
        rows = dst.shape[1] // weight_parts
        span = pl.ds(pl.multiple_of(part * rows, rows), rows)
        return remote(dst.at[1, span], dst.at[1, span], wf_send.at[part], wf_recv.at[part], x_peer)

    for which in (0, 1):
        @pl.when(parity == which)
        def _():
            @pl.loop(0, weight_parts)
            def _(part):
                weight_copy(which, part).start()

    def pair_copy(t, k, rows):
        buf = (xs, gs)[t]
        span = arrive(flip(z, k, experts), c, rows)
        return remote(buf.at[span], buf.at[span], f_send.at[t, k], f_recv.at[t, k], core_peer)

    def own_pair(t, rows):
        src, dst = ((bn, xs), (bg, gs))[t]
        return remote(
            src.at[slots(z, rows)], dst.at[arrive(z, c, rows)], f_send.at[t, 0], f_recv.at[t, 0], core_peer
        )

    def own_local(t, rows):
        src, dst = ((bn, xs), (bg, gs))[t]
        return pltpu.make_async_copy(src.at[slots(z, rows)], dst.at[arrive(z, c, rows)], load.at[t])

    for t in (0, 1):
        sized(z, lambda rows: own_pair(t, rows).start())
        sized(z, lambda rows: own_local(t, rows).start())
    loads = [
        pltpu.make_async_copy(src, dst, load.at[2 + i])
        for i, (src, dst) in enumerate(
            (
                (win_hbm, w_in.at[0]), (wout_hbm, w_out.at[0]),
                (x_hbm, x_ref), (cot_hbm, cot_ref), (aux_hbm, aux_ref),
            )
        )
    ]
    for copy in loads:
        copy.start()

    if hot is not None:
        @pl.when(z != hot)
        def _():
            @pl.loop(0, 2 * experts)
            def _(i):
                rest = pl.ds(pl.multiple_of(i * cap, cap) + cold, cap - cold)
                xs[rest, :] = jnp.zeros((cap - cold, width), BF16)
                gs[rest, :] = jnp.zeros((cap - cold, width), BF16)

        @pl.loop(0, experts)
        def _(e):
            @pl.when(e != hot)
            def _():
                rest = pl.ds(pl.multiple_of(e * cap, cap) + cold, cap - cold)
                ret_n[rest, :] = jnp.zeros((cap - cold, width), BF16)
                ret_g[rest, :] = jnp.zeros((cap - cold, width), BF16)

    for copy in loads:
        copy.wait()
    for t in (0, 1):
        sized(z, lambda rows: own_local(t, rows).wait())

    def other_weights():
        for which in (0, 1):
            @pl.when(parity == which)
            def _():
                @pl.loop(0, weight_parts)
                def _(part):
                    weight_copy(which, part).wait_recv()
                    weight_pass(which, part).start()

                @pl.loop(0, weight_parts)
                def _(part):
                    weight_pass(1 - which, part).wait_recv()
                    weight_copy(which, part).wait_send()
                    weight_pass(which, part).wait_send()

    per_half = hid // hidden_tile

    def rows_in(turn):
        k = turn_k(turn)

        @pl.when(turn > 0)
        def _():
            for t in (0, 1):
                sized(z, lambda rows: z_copy(t, k, rows).wait_recv())
                sized(z, lambda rows: pair_copy(t, k, rows).start())

        for t in (0, 1):
            sized(z, lambda rows: pair_copy(t, k, rows).wait_recv())

    def token_block(turn, first, last):
        source = flip(z, turn_k(turn), experts)
        chunk = pl.ds(pl.multiple_of(source * 2 * cap, 2 * cap), 2 * cap)

        @pl.loop(first, last)
        def _(j):
            half = lax.div(j, per_half)
            cols = pl.ds(pl.multiple_of(lax.rem(j, per_half) * hidden_tile, hidden_tile), hidden_tile)
            pre = dot_nn(xs[chunk, :], w_in[half, :, cols])
            back = dot_nt(gs[chunk, :], w_out[half, cols, :])
            square = pre * pre
            curve = jnp.tanh(pre * (C0 + (C0 * C1) * square))
            low_half = 0.5 + 0.5 * curve
            slope = low_half + pre * (1.0 - curve * curve) * (0.5 * C0 + (1.5 * C0 * C1) * square)
            at = pl.ds(pl.multiple_of(j * hidden_tile, hidden_tile), hidden_tile)
            hs[chunk, at] = (pre * low_half).astype(BF16)
            ps[chunk, at] = (back * slope).astype(BF16)

    def rs_copy(t, k, slot):
        return remote(
            rs_send.at[slot, t], (rs_n, rs_g)[t].at[slots(k)], r_send.at[t, k], r_recv.at[t, k], core_peer
        )

    def back_copy(t, k, rows):
        src, dst = ((rs_n, ret_n), (rs_g, ret_g))[t]
        return remote(
            src.at[slots(k, rows)], dst.at[slots(z, rows)], b_send.at[t, k], b_recv.at[t, k],
            (dp, flip(z, k, experts), h),
        )

    def back_start(turn):
        k = turn_k(turn)
        for t in (0, 1):
            sized(z, lambda rows: back_copy(t, k, rows).start())

    def held(turn):
        if hot is None:
            back_start(turn)
        else:
            @pl.when(z != hot)
            def _():
                back_start(turn)

    def token_sums(turn):
        k = turn_k(turn)
        source = flip(z, k, experts)
        place_in = lax.rem(turn + experts - 1, experts)
        slot = lax.rem(place_in, 2)

        @pl.when(place_in >= 2)
        def _():
            for t in (0, 1):
                rs_copy(t, turn_k(place_in - 1), slot).wait_send()

        @pl.loop(0, 2)
        def _(mine):
            rows = arrive(source, lax.rem(1 + c + mine, 2))
            for t, (values, weights, dot, acc) in enumerate(
                ((hs, w_out, dot_nn, acc_n), (ps, w_in, dot_nt, acc_g))
            ):
                acc = acc.at[pl.ds(0, cap)]
                acc[...] = jnp.zeros_like(acc)

                @pl.loop(0, 2)
                def _(half):
                    cols = pl.ds(pl.multiple_of(half * hid, hid), hid)
                    acc[...] += dot(values[rows, cols], weights[half])

                @pl.when(mine == 0)
                def _():
                    rs_send[slot, t] = acc[...].astype(BF16)
                    rs_copy(t, k, slot).start()

        for t, (acc, got, home) in enumerate(((acc_n, rs_n, ret_n), (acc_g, rs_g, ret_g))):
            rs_copy(t, k, slot).wait_recv()
            both = (acc[pl.ds(0, cap), :] + got[slots(k), :].astype(F32)).astype(BF16)

            @pl.when(turn == 0)
            def _():
                home[slots(z), :] = both

            @pl.when(turn > 0)
            def _():
                got[slots(k), :] = both

    heights = (width // grad_parts, hid // grad_parts)
    subs = tuple(height // PIECE for height in heights)

    def grad_span(t, i, sub=None):
        if sub is None:
            return pl.ds(pl.multiple_of(i * heights[t], heights[t]), heights[t])
        return pl.ds(pl.multiple_of(i * heights[t] + sub * PIECE, PIECE), PIECE)

    def y_copy(t, i, sub):
        src, dst = ((g_in, y_in), (g_out, y_out))[t]
        span, at = grad_span(t, i, sub), i * subs[t] + sub
        return remote(src.at[span], dst.at[span], y_send.at[t, at], y_recv.at[t, at], y_peer)

    def d_copy(t, i, sub):
        src, dst = ((y_in, gb_in), (y_out, gb_out))[t]
        span, at = grad_span(t, i, sub), i * subs[t] + sub
        return remote(src.at[span], dst.at[span], d_send.at[t, at], d_recv.at[t, at], x_peer)

    def d_local(t, i, sub):
        src, dst = ((y_in, ga_in), (y_out, ga_out))[t]
        span, at = grad_span(t, i, sub), i * subs[t] + sub
        return pltpu.make_async_copy(src.at[span], dst.at[span], local.at[t, at])

    accs = (acc_in, acc_n)

    def weight_grad(t, i, half):
        accs[t][...] = jnp.zeros_like(accs[t])
        depth = 2 * cap
        at = pl.ds(pl.multiple_of(half * hid, hid), hid)
        if t:
            at = pl.ds(pl.multiple_of(half * hid + i * heights[1], heights[1]), heights[1])

        @pl.loop(0, experts)
        def _(n):
            rows = pl.ds(pl.multiple_of(n * depth, depth), depth)
            if t == 0:
                accs[t][...] += dot_tn(xs[rows, grad_span(0, i)], ps[rows, at])
            else:
                accs[t][...] += dot_tn(hs[rows, at], gs[rows, :])

    place = hs.at[pl.ds(0, tokens), pl.ds(0, experts * cap)]
    got_n = ps.at[pl.ds(0, tokens), pl.ds(0, width)]
    got_g = ps.at[pl.ds(tokens, tokens), pl.ds(0, width)]
    normed = hs.at[pl.ds(tokens, tokens), pl.ds(0, width)]

    def unbucket():
        @pl.loop(0, tokens // TILE)
        def _(i):
            rows = pl.ds(pl.multiple_of(i * TILE, TILE), TILE)
            slot = aux_ref[rows, experts + 2:experts + 3].astype(jnp.int32)
            lanes = lax.broadcasted_iota(jnp.int32, (TILE, experts * cap), 1)
            place[rows, :] = (slot == lanes).astype(BF16)

        @pl.loop(0, 3)
        def _(n):
            cols = pl.ds(pl.multiple_of(n * (width // 3), width // 3), width // 3)

            @pl.loop(0, tokens // TILE)
            def _(m):
                rows = pl.ds(pl.multiple_of(m * TILE, TILE), TILE)
                got_n[rows, cols] = dot_nn(place[rows, :], ret_n[:, cols]).astype(BF16)
                got_g[rows, cols] = dot_nn(place[rows, :], ret_g[:, cols]).astype(BF16)

    def out_copy(t, i):
        rows = pl.ds(pl.multiple_of(i * SMALL, SMALL), SMALL)
        src, dst = ((act_ref, act_hbm), (ig_ref, ig_hbm))[t]
        return pltpu.make_async_copy(src.at[rows], dst.at[rows], out_sem.at[t, i])

    def tokens_tile(i):
        rows = pl.ds(pl.multiple_of(i * SMALL, SMALL), SMALL)
        aux = aux_ref[rows, :]
        soft, g, inverse = aux[:, :experts], aux[:, experts:experts + 1], aux[:, experts + 1:experts + 2]
        chosen = aux[:, experts + 3:experts + 4].astype(jnp.int32)
        expert_out = got_n[rows, :].astype(F32)
        expert_g = got_g[rows, :].astype(F32)
        x = x_ref[rows, :].astype(F32)
        up = cot_ref[rows, :].astype(F32)
        gain = one_row(gain_ref)
        hits = (chosen == lax.broadcasted_iota(jnp.int32, (SMALL, experts), 1)).astype(F32)
        act_ref[rows, :] = (x + g * expert_out).astype(BF16)
        out_copy(0, i).start()
        gate_g = jnp.sum(up * expert_out, axis=1, keepdims=True)
        logit_g = gate_g * g * (hits - soft)
        logits[rows, :] = logit_g
        normed[rows, :] = (x * inverse * gain).astype(BF16)
        normed_g = expert_g
        for e in range(experts):
            normed_g = normed_g + logit_g[:, e:e + 1] * router_ref[e:e + 1, :].astype(F32)
        total[pl.ds(experts, 1), :] += jnp.sum(normed_g * x * inverse, axis=0, keepdims=True)
        u = gain * normed_g
        dot = jnp.sum(u * x, axis=1, keepdims=True)
        ig_ref[rows, :] = up + inverse * u - x * (inverse * inverse * inverse * dot / width)
        out_copy(1, i).start()

    def router_sum():
        rest = logits[...]
        added = jnp.zeros((experts, width), F32)
        for _ in range(3):
            term = rest.astype(BF16)
            added = added + dot_tn(term, normed[...])
            rest = rest - term.astype(F32)
        total[pl.ds(0, experts), :] = added

    def returned():
        @pl.loop(1, experts)
        def _(turn):
            k = turn_k(turn)
            for t in (0, 1):
                sized(flip(z, k, experts), lambda rows: back_copy(t, k, rows).wait_recv())

    def red_plane_copy(i):
        peer = plane_peer(i, pairs, halves)
        return remote(total, red_plane.at[dp * halves + h], red_send.at[i], red_recv.at[i], peer)

    def red_line_copy(i):
        at = here - 1 + i
        return remote(total, red_line.at[z], red_send.at[at], red_recv.at[at], line_peer(i, experts))

    def token_results():
        returned()
        unbucket()
        total[...] = jnp.zeros_like(total)

        @pl.loop(0, tokens // SMALL)
        def _(i):
            tokens_tile(i)

        router_sum()
        red_plane[dp * halves + h] = total[...]

        @pl.loop(1, here)
        def _(i):
            red_plane_copy(i).start()

    def plane_sum():
        @pl.loop(1, here)
        def _(i):
            red_plane_copy(i).wait()

        added = red_plane[0]
        for i in range(1, here):
            added = added + red_plane[i]
        total[...] = added
        red_line[z] = added

        @pl.loop(1, experts)
        def _(i):
            red_line_copy(i).start()

    plans = (((1, 0), (0, 0), (1, 1), (1, 2), (0, 1), (0, 2)), ((1, 0), (1, 1), (0, 0), (0, 1), (1, 2), (0, 2)))
    late_steps = len(plans[0])

    def planned(t, step, what):
        return sum(jnp.where(step == n, plan[what], 0) for n, plan in enumerate(plans[t]))

    def grad_form(t, step):
        weight_grad(t, planned(t, step, 1), planned(t, step, 0))

    def grad_pass(t, step):
        half, i = planned(t, step, 0), planned(t, step, 1)
        out, got = ((g_in, y_in), (g_out, y_out))[t]

        @pl.when(half == 1)
        def _():
            out[grad_span(t, i), :] = accs[t][...].astype(BF16)

            @pl.loop(0, subs[t])
            def _(sub):
                y_copy(t, i, sub).start()

        @pl.when(half == 0)
        def _():
            @pl.loop(0, subs[t])
            def _(sub):
                if t:
                    @pl.when((step == late_steps - 1) & (sub == subs[1] - 1))
                    def _():
                        token_results()

                span = grad_span(t, i, sub)
                y_copy(t, i, sub).wait_recv()
                mine = accs[t][pl.ds(pl.multiple_of(sub * PIECE, PIECE), PIECE), :]
                got[span, :] = (mine + got[span, :].astype(F32)).astype(BF16)
                if pairs == 2:
                    d_copy(t, i, sub).start()
                d_local(t, i, sub).start()

    @pl.loop(0, experts + 1 + late_steps)
    def _(step):
        late = step - experts - 1

        @pl.when(late >= 0)
        def _():
            grad_form(0, late)

        @pl.when(((step > 2) & (step <= experts)) | (late == 1) | (late == 3))
        def _():
            token_sums(jnp.where(step <= experts, step - 2, jnp.where(late == 1, experts - 1, 0)))

        @pl.when(late == 1)
        def _():
            back_start(experts - 1)

        if hot is not None:
            @pl.when((step > 2) & (step <= experts) & (z == hot))
            def _():
                back_start(step - 2)

        @pl.when(late >= 0)
        def _():
            grad_pass(0, late)

            grad_form(1, late)
            grad_pass(1, late)

        @pl.when(step == 1)
        def _():
            other_weights()

        turn = jnp.where(step < 2, 0, jnp.where(step <= experts, step - 1, experts - 1))

        @pl.when((step != 1) & (step <= experts))
        def _():
            rows_in(turn)

        @pl.when(step <= experts + 1)
        def _():
            token_block(
                turn,
                jnp.where((step == 1) | (step == experts), per_half, 0),
                jnp.where((step == 0) | (step == experts + 1), per_half, 2 * per_half),
            )

        @pl.when(step == experts)
        def _():
            @pl.loop(1, experts - 1)
            def _(earlier):
                held(earlier)

    plane_sum()

    @pl.loop(1, experts)
    def _(i):
        red_line_copy(i).wait()

    added = red_line[0]
    for i in range(1, experts):
        added = added + red_line[i]
    red_ref[...] = added

    @pl.loop(1, experts)
    def _(turn):
        k = turn_k(turn)
        for t in (0, 1):
            sized(flip(z, k, experts), lambda rows: z_copy(t, k, rows).wait_send())
            sized(z, lambda rows: pair_copy(t, k, rows).wait_send())
            sized(z, lambda rows: back_copy(t, k, rows).wait_send())
    for t in (0, 1):
        sized(z, lambda rows: own_pair(t, rows).wait_send())
        for place_in in range(max(0, experts - 2), experts):
            rs_copy(t, turn_k((place_in + 1) % experts), place_in % 2).wait_send()

    @pl.loop(0, tokens // SMALL)
    def _(i):
        for t in (0, 1):
            out_copy(t, i).wait()

    @pl.loop(0, grad_parts)
    def _(i):
        for t in (0, 1):
            @pl.loop(0, subs[t])
            def _(sub):
                y_copy(t, i, sub).wait_send()
                d_local(t, i, sub).wait()
                if pairs == 2:
                    d_copy(t, i, sub).wait()


def finish_kernel(experts, act, ig, red, ai, ao, bi, bo, act_out, ig_out, gain_out, router_out, first_out, second_out):
    act_out[...] = act[...]
    ig_out[...] = ig[...]
    first_out[...] = ai[...].astype(F32) + bi[...].astype(F32)
    second_out[...] = ao[...].astype(F32) + bo[...].astype(F32)

    @pl.when(pl.program_id(0) == 0)
    def _():
        for i in range(gain_out.shape[0]):
            gain_out[i:i + 1, :] = red[experts:experts + 1, i * TILE:(i + 1) * TILE]
        router_out[...] = red[pl.ds(0, experts), :]


def on_device(tokens, route, norm_gain, router_weight, w_in, w_out, cotangent):
    rows, width = tokens.shape
    experts = lax.axis_size("expert")
    pairs = lax.axis_size("dp")
    halves = lax.axis_size("hidden")
    cap = 2 * rows // experts
    hid = w_in.shape[2]
    cold = 16 * (-(-11 * cap // 256))
    hidden_tile = 256
    weight_parts, grad_parts = 12, 3
    grad_pieces = max(width, hid) // PIECE
    slot_rows = experts * cap
    both = 2 * slot_rows
    red_rows = 8 * ((experts + 1 + 7) // 8)
    peers = pairs * halves + experts
    vmem = pl.BlockSpec(memory_space=pltpu.VMEM)
    hbm = pl.BlockSpec(memory_space=pl.ANY)
    sem = pltpu.SemaphoreType.DMA
    shape = jax.ShapeDtypeStruct
    params = functools.partial(pltpu.CompilerParams, has_side_effects=True, vmem_limit_bytes=62 * 1024 * 1024)
    gain_row = norm_gain.reshape(width // TILE, TILE)
    router_rows = router_weight.T

    bn, bg, aux, level = pl.pallas_call(
        functools.partial(prologue_kernel, experts, pairs, halves, cold),
        out_shape=[
            shape((slot_rows, width), BF16),
            shape((slot_rows, width), BF16),
            shape((rows, TILE), F32),
            shape((1,), jnp.int32),
        ],
        in_specs=[hbm, vmem, vmem, vmem, hbm],
        out_specs=[hbm, hbm, vmem, pl.BlockSpec(memory_space=pltpu.SMEM)],
        scratch_shapes=[
            pltpu.VMEM((rows, width), BF16),
            pltpu.VMEM((rows, width), BF16),
            pltpu.VMEM((rows, slot_rows), BF16),
            pltpu.VMEM((TILE, width), BF16),
            pltpu.VMEM((2, rows, TILE), F32),
            pltpu.VMEM((rows, TILE), BF16),
            pltpu.VMEM((2, slot_rows, width), BF16),
            pltpu.VMEM((8, TILE), F32),
            pltpu.VMEM((pairs * halves, 8, TILE), F32),
            pltpu.VMEM((experts, 8, TILE), F32),
            sem((peers,)), sem((peers,)), sem((2,)), sem((2, experts)),
        ],
        compiler_params=params(collective_id=0),
    )(tokens, route.T, gain_row, router_rows, cotangent)

    def block(hot):
        return pl.pallas_call(
            functools.partial(
                block_kernel, experts, pairs, halves, hot, cold, hidden_tile, weight_parts, grad_parts
            ),
            out_shape=[
                shape((rows, width), BF16),
                shape((rows, width), F32),
                shape((red_rows, width), F32),
                shape((width, hid), BF16),
                shape((hid, width), BF16),
                shape((width, hid), BF16),
                shape((hid, width), BF16),
            ],
            in_specs=[hbm, hbm, vmem, vmem, hbm, hbm, hbm, hbm, hbm],
            out_specs=[hbm, hbm, vmem, hbm, hbm, hbm, hbm],
            scratch_shapes=[
                pltpu.VMEM((rows, width), BF16),
                pltpu.VMEM((rows, width), BF16),
                pltpu.VMEM((rows, TILE), F32),
                pltpu.VMEM((2, width, hid), BF16),
                pltpu.VMEM((2, hid, width), BF16),
                pltpu.VMEM((rows, width), BF16),
                pltpu.VMEM((rows, width), F32),
                pltpu.VMEM((both, width), BF16),
                pltpu.VMEM((both, width), BF16),
                pltpu.VMEM((both, 2 * hid), BF16),
                pltpu.VMEM((both, 2 * hid), BF16),
                pltpu.VMEM((width, hid), BF16),
                pltpu.VMEM((hid, width), BF16),
                pltpu.VMEM((width, hid), BF16),
                pltpu.VMEM((hid, width), BF16),
                pltpu.VMEM((2, 2, cap, width), BF16),
                pltpu.VMEM((slot_rows, width), BF16),
                pltpu.VMEM((slot_rows, width), BF16),
                pltpu.VMEM((hid // grad_parts, width), F32),
                pltpu.VMEM((cap, width), F32),
                pltpu.VMEM((width // grad_parts, hid), F32),
                pltpu.VMEM((rows, experts), F32),
                pltpu.VMEM((slot_rows, width), BF16),
                pltpu.VMEM((slot_rows, width), BF16),
                pltpu.VMEM((red_rows, width), F32),
                pltpu.VMEM((pairs * halves, red_rows, width), F32),
                pltpu.VMEM((experts, red_rows, width), F32),
                sem((weight_parts,)), sem((weight_parts,)), sem((weight_parts,)), sem((weight_parts,)),
                sem((2, experts)), sem((2, experts)), sem((2, experts)), sem((2, experts)),
                sem((2, experts)), sem((2, experts)), sem((2, experts)), sem((2, experts)),
                sem((2, grad_pieces)), sem((2, grad_pieces)), sem((2, grad_pieces)), sem((2, grad_pieces)),
                sem((peers,)), sem((peers,)), sem((7,)), sem((2, grad_pieces)), sem((2, rows // SMALL)),
            ],
            compiler_params=params(collective_id=1 + (experts if hot is None else hot)),
        )

    operands = (tokens, aux, gain_row, router_rows, w_in[0], w_out[0], cotangent, bn, bg)
    if experts <= 4:
        branches = [block(e) for e in range(experts)] + [block(None)]
        out = lax.switch(level[0], branches, *operands)
    else:
        out = block(None)(*operands)
    act, ig, red, ga_in, ga_out, gb_in, gb_out = out
    if pairs > 2:
        first, second = lax.psum((ga_in.astype(F32), ga_out.astype(F32)), "dp")
        return act, ig, red[experts], red[:experts].T, first[None], second[None]

    steps = 2

    def blocked(array):
        return pl.BlockSpec((array.shape[0] // steps, array.shape[1]), lambda i: (i, 0))

    def whole(array):
        return pl.BlockSpec(array.shape, lambda i: (0, 0))

    outs = [
        shape((rows, width), BF16),
        shape((rows, width), F32),
        shape((width // TILE, TILE), F32),
        shape((experts, width), F32),
        shape((width, hid), F32),
        shape((hid, width), F32),
    ]
    act, ig, gain_grad, router_grad, first, second = pl.pallas_call(
        functools.partial(finish_kernel, experts),
        grid=(steps,),
        out_shape=outs,
        in_specs=[blocked(act), blocked(ig), whole(red)] + [blocked(a) for a in (ga_in, ga_out, gb_in, gb_out)],
        out_specs=[blocked(outs[0]), blocked(outs[1]), whole(outs[2]), whole(outs[3]), blocked(outs[4]), blocked(outs[5])],
    )(act, ig, red, ga_in, ga_out, gb_in, gb_out)
    return act, ig, gain_grad.reshape(width), router_grad.T, first[None], second[None]


def solution(mesh):
    placed = (
        P(AXES, None),
        P(AXES, None),
        P(),
        P(),
        P("expert", None, "hidden"),
        P("expert", "hidden", None),
        P(AXES, None),
    )
    return jax.shard_map(
        on_device,
        mesh=mesh,
        in_specs=placed,
        out_specs=(
            P(AXES, None),
            P(AXES, None),
            P(),
            P(),
            P("expert", None, "hidden"),
            P("expert", "hidden", None),
        ),
        check_vma=False,
    )
```

```python
import functools

import jax
import jax.numpy as jnp
from jax import lax
from jax.experimental import pallas as pl
from jax.experimental.pallas import tpu as pltpu
from jax.sharding import PartitionSpec as P

HIGHEST = lax.Precision.HIGHEST
MESH = pl.DeviceIdType.MESH
EPSILON = 1e-05
F32 = jnp.float32
BF16 = jnp.bfloat16
AXES = ("dp", "expert", "hidden")
C0 = 0.7978845608
C1 = 0.044715
TILE = 128
PIECE = 128
SMALL = 64


def flip(index, mask, limit):
    out, bit = 0, 1
    while bit < limit:
        a, b = lax.rem(lax.div(index, bit), 2), lax.rem(lax.div(mask, bit), 2)
        out = out + bit * (a + b - 2 * a * b)
        bit *= 2
    return out


def one_row(ref):
    return jnp.concatenate([ref[i:i + 1, :].astype(F32) for i in range(ref.shape[0])], axis=1)


def contract(a, b, left, right, **kwargs):
    return lax.dot_general(a, b, (((left,), (right,)), ((), ())), preferred_element_type=F32, **kwargs)


def dot_nn(a, b):
    return contract(a, b, 1, 0)


def dot_nt(a, b):
    return contract(a, b, 1, 1)


def dot_tn(a, b):
    return contract(a, b, 0, 0)


def remote(src, dst, send, recv, peer):
    return pltpu.make_async_remote_copy(
        src_ref=src, dst_ref=dst, send_sem=send, recv_sem=recv, device_id=peer, device_id_type=MESH
    )


def plane_peer(i, pairs, halves):
    dp, z, h = (lax.axis_index(a) for a in AXES)
    return lax.rem(dp + lax.div(i, halves), pairs), z, lax.rem(h + lax.rem(i, halves), halves)


def line_peer(i, experts):
    dp, z, h = (lax.axis_index(a) for a in AXES)
    return dp, lax.rem(z + i, experts), h


def signal_all(pairs, experts, halves):
    barrier = pltpu.get_barrier_semaphore()

    @pl.loop(1, pairs * halves)
    def _(i):
        pl.semaphore_signal(barrier, inc=1, device_id=plane_peer(i, pairs, halves), device_id_type=MESH)

    @pl.loop(1, experts)
    def _(i):
        pl.semaphore_signal(barrier, inc=1, device_id=line_peer(i, experts), device_id_type=MESH)


def wait_all(pairs, experts, halves):
    pl.semaphore_wait(pltpu.get_barrier_semaphore(), pairs * halves + experts - 2)


def prologue_kernel(
    experts, pairs, halves, cold,
    x_hbm, route_ref, gain_ref, router_ref, cot_hbm,
    bn_out, bg_out, aux_ref, level_ref,
    x_ref, cot_ref, place, router, ranks, marks, stage, counts, count_in, line_in, send, recv, load, local,
):
    tokens, width = x_ref.shape
    cap = bn_out.shape[0] // experts
    signal_all(pairs, experts, halves)
    loads = [
        pltpu.make_async_copy(src, dst, load.at[i])
        for i, (src, dst) in enumerate(((x_hbm, x_ref), (cot_hbm, cot_ref)))
    ]
    for copy in loads:
        copy.start()

    lane = lax.broadcasted_iota(jnp.int32, (tokens, TILE), 1)
    chosen = jnp.transpose(jnp.broadcast_to(route_ref[...].astype(F32), (TILE, tokens)))
    onehot = (chosen.astype(jnp.int32) == lane).astype(F32)
    counts[...] = jnp.broadcast_to(jnp.sum(onehot, axis=0, keepdims=True), (8, TILE))
    here = pairs * halves

    def plane_copy(i):
        return remote(counts, count_in.at[i], send.at[i], recv.at[i], plane_peer(i, pairs, halves))

    def line_copy(i):
        at = here - 1 + i
        return remote(count_in.at[0], line_in.at[i], send.at[at], recv.at[at], line_peer(i, experts))

    wait_all(pairs, experts, halves)

    @pl.loop(1, here)
    def _(i):
        plane_copy(i).start()

    ranks[0] = chosen
    marks[...] = onehot.astype(BF16)

    @pl.loop(0, tokens // TILE)
    def _(i):
        rows = pl.ds(pl.multiple_of(i * TILE, TILE), TILE)
        before = (
            lax.broadcasted_iota(jnp.int32, (TILE, tokens), 1)
            < lax.broadcasted_iota(jnp.int32, (TILE, tokens), 0) + i * TILE
        ).astype(BF16)
        rank = jnp.sum(dot_nn(before, marks[...]) * marks[rows, :].astype(F32), axis=1, keepdims=True)
        ranks[1, rows, :] = ranks[0, rows, :] * cap + rank

    router[...] = jnp.zeros_like(router)
    router[pl.ds(0, experts), :] = router_ref[...]

    for copy in loads:
        copy.wait()

    @pl.loop(0, tokens // TILE)
    def _(i):
        rows = pl.ds(pl.multiple_of(i * TILE, TILE), TILE)
        x = x_ref[rows, :].astype(F32)
        inverse = lax.rsqrt(jnp.mean(x * x, axis=1, keepdims=True) + EPSILON)
        low = (x * inverse * one_row(gain_ref)).astype(BF16)
        x_ref[rows, :] = low
        lanes = lax.broadcasted_iota(jnp.int32, (TILE, TILE), 1)
        expert, slot = ranks[0, rows, :], ranks[1, rows, :]
        logits = jnp.where(lanes < experts, dot_nt(low, router[...]), -jnp.inf)
        shifted = jnp.exp(logits - jnp.max(logits, axis=1, keepdims=True))
        soft = shifted / jnp.sum(shifted, axis=1, keepdims=True)
        gate = jnp.sum(jnp.where(expert.astype(jnp.int32) == lanes, soft, 0.0), axis=1, keepdims=True)
        cot_ref[rows, :] = (gate * cot_ref[rows, :].astype(F32)).astype(BF16)
        aux = jnp.where(lanes == experts, gate, soft)
        aux = jnp.where(lanes == experts + 1, inverse, aux)
        aux = jnp.where(lanes == experts + 2, slot, aux)
        aux_ref[rows, :] = jnp.where(lanes == experts + 3, expert, aux)
        slot_int = slot.astype(jnp.int32)

        @pl.loop(0, experts * cap // TILE)
        def _(j):
            at = pl.ds(pl.multiple_of(j * TILE, TILE), TILE)
            place[rows, at] = (slot_int == lanes + j * TILE).astype(BF16)

    most = counts[...]
    for i in range(1, here):
        plane_copy(i).wait_recv()
        most = jnp.maximum(most, count_in[i])
    count_in[0] = most

    @pl.loop(1, experts)
    def _(i):
        line_copy(i).start()

    def out_copy(t, e):
        span = pl.ds(pl.multiple_of(e * cap, cap), cap)
        return pltpu.make_async_copy(stage.at[t, span], (bn_out, bg_out)[t].at[span], local.at[t, e])

    @pl.loop(0, experts)
    def _(e):
        span = pl.ds(pl.multiple_of(e * cap, cap), cap)
        for t, values in enumerate((x_ref, cot_ref)):
            stage[t, span, :] = dot_tn(place[:, span], values[...]).astype(BF16)
            out_copy(t, e).start()

    most = count_in[0]
    for i in range(1, experts):
        line_copy(i).wait_recv()
        most = jnp.maximum(most, line_in[i])
    lanes = lax.broadcasted_iota(jnp.int32, (8, TILE), 1)
    rows = lax.broadcasted_iota(jnp.int32, (8, TILE), 0)
    over = jnp.where((most > cold) & (rows == 0), 1.0, 0.0)
    crowded = jnp.sum(over)
    which = jnp.sum(over * lanes.astype(F32))
    level_ref[0] = jnp.where(crowded <= 1.0, which, float(experts)).astype(jnp.int32)

    @pl.loop(1, here)
    def _(i):
        plane_copy(i).wait_send()

    @pl.loop(1, experts)
    def _(i):
        line_copy(i).wait_send()

    @pl.loop(0, experts)
    def _(e):
        for t in (0, 1):
            out_copy(t, e).wait()


def block_kernel(
    experts, pairs, halves, hot, cold, hidden_tile, weight_parts, grad_parts,
    x_hbm, aux_hbm, gain_ref, router_ref, win_hbm, wout_hbm, cot_hbm, bn, bg,
    act_hbm, ig_hbm, red_ref, ga_in, ga_out, gb_in, gb_out,
    x_ref, cot_ref, aux_ref, w_in, w_out, act_ref, ig_ref,
    xs, gs, hs, ps, g_in, g_out, y_in, y_out,
    rs_send, rs_n, rs_g, acc_n, acc_g, acc_in, logits, ret_n, ret_g, total, red_plane, red_line,
    w_send, w_recv, wf_send, wf_recv, z_send, z_recv, f_send, f_recv, r_send, r_recv,
    b_send, b_recv, y_send, y_recv, d_send, d_recv, red_send, red_recv, load, local, out_sem,
):
    tokens, width = x_ref.shape
    hid = w_in.shape[2]
    cap = bn.shape[0] // experts
    dp, z, h = (lax.axis_index(a) for a in AXES)
    c = lax.rem(h, 2)
    parity = lax.rem(dp, 2)
    core_peer = (dp, z, flip(h, 1, halves))
    y_peer = (dp, z, flip(h, 2, halves))
    x_peer = (flip(dp, 1, pairs), z, h)
    here = pairs * halves
    signal_all(pairs, experts, halves)
    wait_all(pairs, experts, halves)

    def sized(e, act):
        if hot is None:
            act(cap)
        else:
            @pl.when(e == hot)
            def _():
                act(cap)

            @pl.when(e != hot)
            def _():
                act(cold)

    def slots(e, rows=cap):
        return pl.ds(pl.multiple_of(e * cap, cap), rows)

    def arrive(source, core, rows=cap):
        return pl.ds(pl.multiple_of((source * 2 + core) * cap, cap), rows)

    def turn_k(turn):
        return flip(turn, lax.div(turn, 2), experts)

    def z_copy(t, k, rows):
        src, dst = ((bn, xs), (bg, gs))[t]
        e = flip(z, k, experts)
        return remote(
            src.at[slots(e, rows)], dst.at[arrive(z, c, rows)], z_send.at[t, k], z_recv.at[t, k], (dp, e, h)
        )

    def z_start(t, k):
        sized(flip(z, k, experts), lambda rows: z_copy(t, k, rows).start())

    order = sorted(range(1, experts), key=lambda k: (k != experts - 1, k))
    for k in order:
        for t in (0, 1):
            z_start(t, k)

    mats = ((win_hbm, w_in), (wout_hbm, w_out))

    def weight_copy(which, part):
        src, dst = mats[which]
        rows = src.shape[0] // weight_parts
        span = pl.ds(pl.multiple_of(part * rows, rows), rows)
        return remote(src.at[span], dst.at[1, span], w_send.at[part], w_recv.at[part], y_peer)

    def weight_pass(which, part):
        dst = mats[which][1]
        rows = dst.shape[1] // weight_parts
        span = pl.ds(pl.multiple_of(part * rows, rows), rows)
        return remote(dst.at[1, span], dst.at[1, span], wf_send.at[part], wf_recv.at[part], x_peer)

    for which in (0, 1):
        @pl.when(parity == which)
        def _():
            @pl.loop(0, weight_parts)
            def _(part):
                weight_copy(which, part).start()

    def pair_copy(t, k, rows):
        buf = (xs, gs)[t]
        span = arrive(flip(z, k, experts), c, rows)
        return remote(buf.at[span], buf.at[span], f_send.at[t, k], f_recv.at[t, k], core_peer)

    def own_pair(t, rows):
        src, dst = ((bn, xs), (bg, gs))[t]
        return remote(
            src.at[slots(z, rows)], dst.at[arrive(z, c, rows)], f_send.at[t, 0], f_recv.at[t, 0], core_peer
        )

    def own_local(t, rows):
        src, dst = ((bn, xs), (bg, gs))[t]
        return pltpu.make_async_copy(src.at[slots(z, rows)], dst.at[arrive(z, c, rows)], load.at[t])

    for t in (0, 1):
        sized(z, lambda rows: own_pair(t, rows).start())
        sized(z, lambda rows: own_local(t, rows).start())
    loads = [
        pltpu.make_async_copy(src, dst, load.at[2 + i])
        for i, (src, dst) in enumerate(
            (
                (win_hbm, w_in.at[0]), (wout_hbm, w_out.at[0]),
                (x_hbm, x_ref), (cot_hbm, cot_ref), (aux_hbm, aux_ref),
            )
        )
    ]
    for copy in loads:
        copy.start()

    if hot is not None:
        @pl.when(z != hot)
        def _():
            @pl.loop(0, 2 * experts)
            def _(i):
                rest = pl.ds(pl.multiple_of(i * cap, cap) + cold, cap - cold)
                xs[rest, :] = jnp.zeros((cap - cold, width), BF16)
                gs[rest, :] = jnp.zeros((cap - cold, width), BF16)

        @pl.loop(0, experts)
        def _(e):
            @pl.when(e != hot)
            def _():
                rest = pl.ds(pl.multiple_of(e * cap, cap) + cold, cap - cold)
                ret_n[rest, :] = jnp.zeros((cap - cold, width), BF16)
                ret_g[rest, :] = jnp.zeros((cap - cold, width), BF16)

    for copy in loads:
        copy.wait()
    for t in (0, 1):
        sized(z, lambda rows: own_local(t, rows).wait())

    def other_weights():
        for which in (0, 1):
            @pl.when(parity == which)
            def _():
                @pl.loop(0, weight_parts)
                def _(part):
                    weight_copy(which, part).wait_recv()
                    weight_pass(which, part).start()

                @pl.loop(0, weight_parts)
                def _(part):
                    weight_pass(1 - which, part).wait_recv()
                    weight_copy(which, part).wait_send()
                    weight_pass(which, part).wait_send()

    per_half = hid // hidden_tile

    def rows_in(turn):
        k = turn_k(turn)

        @pl.when(turn > 0)
        def _():
            for t in (0, 1):
                sized(z, lambda rows: z_copy(t, k, rows).wait_recv())
                sized(z, lambda rows: pair_copy(t, k, rows).start())

        for t in (0, 1):
            sized(z, lambda rows: pair_copy(t, k, rows).wait_recv())

    def token_block(turn, first, last):
        source = flip(z, turn_k(turn), experts)
        chunk = pl.ds(pl.multiple_of(source * 2 * cap, 2 * cap), 2 * cap)

        @pl.loop(first, last)
        def _(j):
            half = lax.div(j, per_half)
            cols = pl.ds(pl.multiple_of(lax.rem(j, per_half) * hidden_tile, hidden_tile), hidden_tile)
            pre = dot_nn(xs[chunk, :], w_in[half, :, cols])
            back = dot_nt(gs[chunk, :], w_out[half, cols, :])
            square = pre * pre
            curve = jnp.tanh(pre * (C0 + (C0 * C1) * square))
            low_half = 0.5 + 0.5 * curve
            slope = low_half + pre * (1.0 - curve * curve) * (0.5 * C0 + (1.5 * C0 * C1) * square)
            at = pl.ds(pl.multiple_of(j * hidden_tile, hidden_tile), hidden_tile)
            hs[chunk, at] = (pre * low_half).astype(BF16)
            ps[chunk, at] = (back * slope).astype(BF16)

    def rs_copy(t, k, slot):
        return remote(
            rs_send.at[slot, t], (rs_n, rs_g)[t].at[slots(k)], r_send.at[t, k], r_recv.at[t, k], core_peer
        )

    def back_copy(t, k, rows):
        src, dst = ((rs_n, ret_n), (rs_g, ret_g))[t]
        return remote(
            src.at[slots(k, rows)], dst.at[slots(z, rows)], b_send.at[t, k], b_recv.at[t, k],
            (dp, flip(z, k, experts), h),
        )

    def back_start(turn):
        k = turn_k(turn)
        for t in (0, 1):
            sized(z, lambda rows: back_copy(t, k, rows).start())

    def held(turn):
        if hot is None:
            back_start(turn)
        else:
            @pl.when(z != hot)
            def _():
                back_start(turn)

    def token_sums(turn):
        k = turn_k(turn)
        source = flip(z, k, experts)
        place_in = lax.rem(turn + experts - 1, experts)
        slot = lax.rem(place_in, 2)

        @pl.when(place_in >= 2)
        def _():
            for t in (0, 1):
                rs_copy(t, turn_k(place_in - 1), slot).wait_send()

        @pl.loop(0, 2)
        def _(mine):
            rows = arrive(source, lax.rem(1 + c + mine, 2))
            for t, (values, weights, dot, acc) in enumerate(
                ((hs, w_out, dot_nn, acc_n), (ps, w_in, dot_nt, acc_g))
            ):
                acc = acc.at[pl.ds(0, cap)]
                acc[...] = jnp.zeros_like(acc)

                @pl.loop(0, 2)
                def _(half):
                    cols = pl.ds(pl.multiple_of(half * hid, hid), hid)
                    acc[...] += dot(values[rows, cols], weights[half])

                @pl.when(mine == 0)
                def _():
                    rs_send[slot, t] = acc[...].astype(BF16)
                    rs_copy(t, k, slot).start()

        for t, (acc, got, home) in enumerate(((acc_n, rs_n, ret_n), (acc_g, rs_g, ret_g))):
            rs_copy(t, k, slot).wait_recv()
            both = (acc[pl.ds(0, cap), :] + got[slots(k), :].astype(F32)).astype(BF16)

            @pl.when(turn == 0)
            def _():
                home[slots(z), :] = both

            @pl.when(turn > 0)
            def _():
                got[slots(k), :] = both

    heights = (width // grad_parts, hid // grad_parts)
    subs = tuple(height // PIECE for height in heights)

    def grad_span(t, i, sub=None):
        if sub is None:
            return pl.ds(pl.multiple_of(i * heights[t], heights[t]), heights[t])
        return pl.ds(pl.multiple_of(i * heights[t] + sub * PIECE, PIECE), PIECE)

    def y_copy(t, i, sub):
        src, dst = ((g_in, y_in), (g_out, y_out))[t]
        span, at = grad_span(t, i, sub), i * subs[t] + sub
        return remote(src.at[span], dst.at[span], y_send.at[t, at], y_recv.at[t, at], y_peer)

    def d_copy(t, i, sub):
        src, dst = ((y_in, gb_in), (y_out, gb_out))[t]
        span, at = grad_span(t, i, sub), i * subs[t] + sub
        return remote(src.at[span], dst.at[span], d_send.at[t, at], d_recv.at[t, at], x_peer)

    def d_local(t, i, sub):
        src, dst = ((y_in, ga_in), (y_out, ga_out))[t]
        span, at = grad_span(t, i, sub), i * subs[t] + sub
        return pltpu.make_async_copy(src.at[span], dst.at[span], local.at[t, at])

    accs = (acc_in, acc_n)

    def weight_grad(t, i, half):
        accs[t][...] = jnp.zeros_like(accs[t])
        depth = 2 * cap
        at = pl.ds(pl.multiple_of(half * hid, hid), hid)
        if t:
            at = pl.ds(pl.multiple_of(half * hid + i * heights[1], heights[1]), heights[1])

        @pl.loop(0, experts)
        def _(n):
            rows = pl.ds(pl.multiple_of(n * depth, depth), depth)
            if t == 0:
                accs[t][...] += dot_tn(xs[rows, grad_span(0, i)], ps[rows, at])
            else:
                accs[t][...] += dot_tn(hs[rows, at], gs[rows, :])

    place = hs.at[pl.ds(0, tokens), pl.ds(0, experts * cap)]
    got_n = ps.at[pl.ds(0, tokens), pl.ds(0, width)]
    got_g = ps.at[pl.ds(tokens, tokens), pl.ds(0, width)]
    normed = hs.at[pl.ds(tokens, tokens), pl.ds(0, width)]

    def unbucket():
        @pl.loop(0, tokens // TILE)
        def _(i):
            rows = pl.ds(pl.multiple_of(i * TILE, TILE), TILE)
            slot = aux_ref[rows, experts + 2:experts + 3].astype(jnp.int32)
            lanes = lax.broadcasted_iota(jnp.int32, (TILE, experts * cap), 1)
            place[rows, :] = (slot == lanes).astype(BF16)

        @pl.loop(0, 3)
        def _(n):
            cols = pl.ds(pl.multiple_of(n * (width // 3), width // 3), width // 3)

            @pl.loop(0, tokens // TILE)
            def _(m):
                rows = pl.ds(pl.multiple_of(m * TILE, TILE), TILE)
                got_n[rows, cols] = dot_nn(place[rows, :], ret_n[:, cols]).astype(BF16)
                got_g[rows, cols] = dot_nn(place[rows, :], ret_g[:, cols]).astype(BF16)

    def out_copy(t, i):
        rows = pl.ds(pl.multiple_of(i * SMALL, SMALL), SMALL)
        src, dst = ((act_ref, act_hbm), (ig_ref, ig_hbm))[t]
        return pltpu.make_async_copy(src.at[rows], dst.at[rows], out_sem.at[t, i])

    def tokens_tile(i):
        rows = pl.ds(pl.multiple_of(i * SMALL, SMALL), SMALL)
        aux = aux_ref[rows, :]
        soft, g, inverse = aux[:, :experts], aux[:, experts:experts + 1], aux[:, experts + 1:experts + 2]
        chosen = aux[:, experts + 3:experts + 4].astype(jnp.int32)
        expert_out = got_n[rows, :].astype(F32)
        expert_g = got_g[rows, :].astype(F32)
        x = x_ref[rows, :].astype(F32)
        up = cot_ref[rows, :].astype(F32)
        gain = one_row(gain_ref)
        hits = (chosen == lax.broadcasted_iota(jnp.int32, (SMALL, experts), 1)).astype(F32)
        act_ref[rows, :] = (x + g * expert_out).astype(BF16)
        out_copy(0, i).start()
        gate_g = jnp.sum(up * expert_out, axis=1, keepdims=True)
        logit_g = gate_g * g * (hits - soft)
        logits[rows, :] = logit_g
        normed[rows, :] = (x * inverse * gain).astype(BF16)
        normed_g = expert_g
        for e in range(experts):
            normed_g = normed_g + logit_g[:, e:e + 1] * router_ref[e:e + 1, :].astype(F32)
        total[pl.ds(experts, 1), :] += jnp.sum(normed_g * x * inverse, axis=0, keepdims=True)
        u = gain * normed_g
        dot = jnp.sum(u * x, axis=1, keepdims=True)
        ig_ref[rows, :] = up + inverse * u - x * (inverse * inverse * inverse * dot / width)
        out_copy(1, i).start()

    def router_sum():
        rest = logits[...]
        added = jnp.zeros((experts, width), F32)
        for _ in range(3):
            term = rest.astype(BF16)
            added = added + dot_tn(term, normed[...])
            rest = rest - term.astype(F32)
        total[pl.ds(0, experts), :] = added

    def returned():
        @pl.loop(1, experts)
        def _(turn):
            k = turn_k(turn)
            for t in (0, 1):
                sized(flip(z, k, experts), lambda rows: back_copy(t, k, rows).wait_recv())

    def red_plane_copy(i):
        peer = plane_peer(i, pairs, halves)
        return remote(total, red_plane.at[dp * halves + h], red_send.at[i], red_recv.at[i], peer)

    def red_line_copy(i):
        at = here - 1 + i
        return remote(total, red_line.at[z], red_send.at[at], red_recv.at[at], line_peer(i, experts))

    def token_results():
        returned()
        unbucket()
        total[...] = jnp.zeros_like(total)

        @pl.loop(0, tokens // SMALL)
        def _(i):
            tokens_tile(i)

        router_sum()
        red_plane[dp * halves + h] = total[...]

        @pl.loop(1, here)
        def _(i):
            red_plane_copy(i).start()

    def plane_sum():
        @pl.loop(1, here)
        def _(i):
            red_plane_copy(i).wait()

        added = red_plane[0]
        for i in range(1, here):
            added = added + red_plane[i]
        total[...] = added
        red_line[z] = added

        @pl.loop(1, experts)
        def _(i):
            red_line_copy(i).start()

    plans = (((1, 0), (0, 0), (1, 1), (1, 2), (0, 1), (0, 2)), ((1, 0), (1, 1), (0, 0), (0, 1), (1, 2), (0, 2)))
    late_steps = len(plans[0])

    def planned(t, step, what):
        return sum(jnp.where(step == n, plan[what], 0) for n, plan in enumerate(plans[t]))

    def grad_form(t, step):
        weight_grad(t, planned(t, step, 1), planned(t, step, 0))

    def grad_pass(t, step):
        half, i = planned(t, step, 0), planned(t, step, 1)
        out, got = ((g_in, y_in), (g_out, y_out))[t]

        @pl.when(half == 1)
        def _():
            out[grad_span(t, i), :] = accs[t][...].astype(BF16)

            @pl.loop(0, subs[t])
            def _(sub):
                y_copy(t, i, sub).start()

        @pl.when(half == 0)
        def _():
            @pl.loop(0, subs[t])
            def _(sub):
                if t:
                    @pl.when((step == late_steps - 1) & (sub == subs[1] - 1))
                    def _():
                        token_results()

                span = grad_span(t, i, sub)
                y_copy(t, i, sub).wait_recv()
                mine = accs[t][pl.ds(pl.multiple_of(sub * PIECE, PIECE), PIECE), :]
                got[span, :] = (mine + got[span, :].astype(F32)).astype(BF16)
                if pairs == 2:
                    d_copy(t, i, sub).start()
                d_local(t, i, sub).start()

    @pl.loop(0, experts + 1 + late_steps)
    def _(step):
        late = step - experts - 1

        @pl.when(late >= 0)
        def _():
            grad_form(0, late)

        @pl.when(((step > 2) & (step <= experts)) | (late == 1) | (late == 3))
        def _():
            token_sums(jnp.where(step <= experts, step - 2, jnp.where(late == 1, experts - 1, 0)))

        @pl.when(late == 1)
        def _():
            back_start(experts - 1)

        if hot is not None:
            @pl.when((step > 2) & (step <= experts) & (z == hot))
            def _():
                back_start(step - 2)

        @pl.when(late >= 0)
        def _():
            grad_pass(0, late)

            grad_form(1, late)
            grad_pass(1, late)

        @pl.when(step == 1)
        def _():
            other_weights()

        turn = jnp.where(step < 2, 0, jnp.where(step <= experts, step - 1, experts - 1))

        @pl.when((step != 1) & (step <= experts))
        def _():
            rows_in(turn)

        @pl.when(step <= experts + 1)
        def _():
            token_block(
                turn,
                jnp.where((step == 1) | (step == experts), per_half, 0),
                jnp.where((step == 0) | (step == experts + 1), per_half, 2 * per_half),
            )

        @pl.when(step == experts)
        def _():
            @pl.loop(1, experts - 1)
            def _(earlier):
                held(earlier)

    plane_sum()

    @pl.loop(1, experts)
    def _(i):
        red_line_copy(i).wait()

    added = red_line[0]
    for i in range(1, experts):
        added = added + red_line[i]
    red_ref[...] = added

    @pl.loop(1, experts)
    def _(turn):
        k = turn_k(turn)
        for t in (0, 1):
            sized(flip(z, k, experts), lambda rows: z_copy(t, k, rows).wait_send())
            sized(z, lambda rows: pair_copy(t, k, rows).wait_send())
            sized(z, lambda rows: back_copy(t, k, rows).wait_send())
    for t in (0, 1):
        sized(z, lambda rows: own_pair(t, rows).wait_send())
        for place_in in range(max(0, experts - 2), experts):
            rs_copy(t, turn_k((place_in + 1) % experts), place_in % 2).wait_send()

    @pl.loop(0, tokens // SMALL)
    def _(i):
        for t in (0, 1):
            out_copy(t, i).wait()

    @pl.loop(0, grad_parts)
    def _(i):
        for t in (0, 1):
            @pl.loop(0, subs[t])
            def _(sub):
                y_copy(t, i, sub).wait_send()
                d_local(t, i, sub).wait()
                if pairs == 2:
                    d_copy(t, i, sub).wait()


def finish_kernel(experts, act, ig, red, ai, ao, bi, bo, act_out, ig_out, gain_out, router_out, first_out, second_out):
    act_out[...] = act[...]
    ig_out[...] = ig[...]
    first_out[...] = ai[...].astype(F32) + bi[...].astype(F32)
    second_out[...] = ao[...].astype(F32) + bo[...].astype(F32)

    @pl.when(pl.program_id(0) == 0)
    def _():
        for i in range(gain_out.shape[0]):
            gain_out[i:i + 1, :] = red[experts:experts + 1, i * TILE:(i + 1) * TILE]
        router_out[...] = red[pl.ds(0, experts), :]


def on_device(tokens, route, norm_gain, router_weight, w_in, w_out, cotangent):
    rows, width = tokens.shape
    experts = lax.axis_size("expert")
    pairs = lax.axis_size("dp")
    halves = lax.axis_size("hidden")
    cap = 2 * rows // experts
    hid = w_in.shape[2]
    cold = 16 * (-(-11 * cap // 256))
    hidden_tile = 256
    weight_parts, grad_parts = 12, 3
    grad_pieces = max(width, hid) // PIECE
    slot_rows = experts * cap
    both = 2 * slot_rows
    red_rows = 8 * ((experts + 1 + 7) // 8)
    peers = pairs * halves + experts
    vmem = pl.BlockSpec(memory_space=pltpu.VMEM)
    hbm = pl.BlockSpec(memory_space=pl.ANY)
    sem = pltpu.SemaphoreType.DMA
    shape = jax.ShapeDtypeStruct
    params = functools.partial(pltpu.CompilerParams, has_side_effects=True, vmem_limit_bytes=62 * 1024 * 1024)
    gain_row = norm_gain.reshape(width // TILE, TILE)
    router_rows = router_weight.T

    bn, bg, aux, level = pl.pallas_call(
        functools.partial(prologue_kernel, experts, pairs, halves, cold),
        out_shape=[
            shape((slot_rows, width), BF16),
            shape((slot_rows, width), BF16),
            shape((rows, TILE), F32),
            shape((1,), jnp.int32),
        ],
        in_specs=[hbm, vmem, vmem, vmem, hbm],
        out_specs=[hbm, hbm, vmem, pl.BlockSpec(memory_space=pltpu.SMEM)],
        scratch_shapes=[
            pltpu.VMEM((rows, width), BF16),
            pltpu.VMEM((rows, width), BF16),
            pltpu.VMEM((rows, slot_rows), BF16),
            pltpu.VMEM((TILE, width), BF16),
            pltpu.VMEM((2, rows, TILE), F32),
            pltpu.VMEM((rows, TILE), BF16),
            pltpu.VMEM((2, slot_rows, width), BF16),
            pltpu.VMEM((8, TILE), F32),
            pltpu.VMEM((pairs * halves, 8, TILE), F32),
            pltpu.VMEM((experts, 8, TILE), F32),
            sem((peers,)), sem((peers,)), sem((2,)), sem((2, experts)),
        ],
        compiler_params=params(collective_id=0),
    )(tokens, route.T, gain_row, router_rows, cotangent)

    def block(hot):
        return pl.pallas_call(
            functools.partial(
                block_kernel, experts, pairs, halves, hot, cold, hidden_tile, weight_parts, grad_parts
            ),
            out_shape=[
                shape((rows, width), BF16),
                shape((rows, width), F32),
                shape((red_rows, width), F32),
                shape((width, hid), BF16),
                shape((hid, width), BF16),
                shape((width, hid), BF16),
                shape((hid, width), BF16),
            ],
            in_specs=[hbm, hbm, vmem, vmem, hbm, hbm, hbm, hbm, hbm],
            out_specs=[hbm, hbm, vmem, hbm, hbm, hbm, hbm],
            scratch_shapes=[
                pltpu.VMEM((rows, width), BF16),
                pltpu.VMEM((rows, width), BF16),
                pltpu.VMEM((rows, TILE), F32),
                pltpu.VMEM((2, width, hid), BF16),
                pltpu.VMEM((2, hid, width), BF16),
                pltpu.VMEM((rows, width), BF16),
                pltpu.VMEM((rows, width), F32),
                pltpu.VMEM((both, width), BF16),
                pltpu.VMEM((both, width), BF16),
                pltpu.VMEM((both, 2 * hid), BF16),
                pltpu.VMEM((both, 2 * hid), BF16),
                pltpu.VMEM((width, hid), BF16),
                pltpu.VMEM((hid, width), BF16),
                pltpu.VMEM((width, hid), BF16),
                pltpu.VMEM((hid, width), BF16),
                pltpu.VMEM((2, 2, cap, width), BF16),
                pltpu.VMEM((slot_rows, width), BF16),
                pltpu.VMEM((slot_rows, width), BF16),
                pltpu.VMEM((hid // grad_parts, width), F32),
                pltpu.VMEM((cap, width), F32),
                pltpu.VMEM((width // grad_parts, hid), F32),
                pltpu.VMEM((rows, experts), F32),
                pltpu.VMEM((slot_rows, width), BF16),
                pltpu.VMEM((slot_rows, width), BF16),
                pltpu.VMEM((red_rows, width), F32),
                pltpu.VMEM((pairs * halves, red_rows, width), F32),
                pltpu.VMEM((experts, red_rows, width), F32),
                sem((weight_parts,)), sem((weight_parts,)), sem((weight_parts,)), sem((weight_parts,)),
                sem((2, experts)), sem((2, experts)), sem((2, experts)), sem((2, experts)),
                sem((2, experts)), sem((2, experts)), sem((2, experts)), sem((2, experts)),
                sem((2, grad_pieces)), sem((2, grad_pieces)), sem((2, grad_pieces)), sem((2, grad_pieces)),
                sem((peers,)), sem((peers,)), sem((7,)), sem((2, grad_pieces)), sem((2, rows // SMALL)),
            ],
            compiler_params=params(collective_id=1 + (experts if hot is None else hot)),
        )

    operands = (tokens, aux, gain_row, router_rows, w_in[0], w_out[0], cotangent, bn, bg)
    if experts <= 4:
        branches = [block(e) for e in range(experts)] + [block(None)]
        out = lax.switch(level[0], branches, *operands)
    else:
        out = block(None)(*operands)
    act, ig, red, ga_in, ga_out, gb_in, gb_out = out
    if pairs > 2:
        first, second = lax.psum((ga_in.astype(F32), ga_out.astype(F32)), "dp")
        return act, ig, red[experts], red[:experts].T, first[None], second[None]

    steps = 2

    def blocked(array):
        return pl.BlockSpec((array.shape[0] // steps, array.shape[1]), lambda i: (i, 0))

    def whole(array):
        return pl.BlockSpec(array.shape, lambda i: (0, 0))

    outs = [
        shape((rows, width), BF16),
        shape((rows, width), F32),
        shape((width // TILE, TILE), F32),
        shape((experts, width), F32),
        shape((width, hid), F32),
        shape((hid, width), F32),
    ]
    act, ig, gain_grad, router_grad, first, second = pl.pallas_call(
        functools.partial(finish_kernel, experts),
        grid=(steps,),
        out_shape=outs,
        in_specs=[blocked(act), blocked(ig), whole(red)] + [blocked(a) for a in (ga_in, ga_out, gb_in, gb_out)],
        out_specs=[blocked(outs[0]), blocked(outs[1]), whole(outs[2]), whole(outs[3]), blocked(outs[4]), blocked(outs[5])],
    )(act, ig, red, ga_in, ga_out, gb_in, gb_out)
    return act, ig, gain_grad.reshape(width), router_grad.T, first[None], second[None]


def solution(mesh):
    placed = (
        P(AXES, None),
        P(AXES, None),
        P(),
        P(),
        P("expert", None, "hidden"),
        P("expert", "hidden", None),
        P(AXES, None),
    )
    return jax.shard_map(
        on_device,
        mesh=mesh,
        in_specs=placed,
        out_specs=(
            P(AXES, None),
            P(AXES, None),
            P(),
            P(),
            P("expert", None, "hidden"),
            P("expert", "hidden", None),
        ),
        check_vma=False,
    )
```
